32 devices in a mesh: crow: 8 (over z, x), ccol: 4 (over y, core).
Axes of the slice: x: 2, y: 2, z: 4, core: 2. Of those that a mesh axis runs over, the one named last changes fastest.
Arguments:
- sketch: float32 [131072, 512], P(('crow', 'ccol')), may hold values from -120 to 120, as said below
Outputs:
- posterior_basis: float32 [131072, 512], P(('crow', 'ccol'))
- mean_log_eigen: float32 [], replicated
The draws below stay inside these ranges and needn't reach their ends.
Inputs may be any that keep to these rules, and one draw needn't show every extreme that they name: Entries of the sketch are real numbers of either sign.
All inputs are finite; a program needn't handle non-finite values.
Results may differ from the reference program's by a relative error of at most 0.0003.
Values sent between devices are 32-bit elements; how exact they have to be, the bound alone decides.
No kernel may reach another device: no remote copies, remote signals or barrier semaphores. Data moves between devices by JAX's collectives and lax.ppermute only.
A program may use at most 128 MiB of HBM per device.

```python
import math
import jax
import jax.numpy as jnp
from jax import lax

K = 512
ROWS = 131072


def draw_sketch(key, part):
    key = jax.random.fold_in(key, 7)
    keys = jax.random.split(key, 3)
    noise = jnp.clip(jax.random.normal(keys[0], (ROWS, K), jnp.float32), -5.0, 5.0)
    mixed = noise + 0.7 * jnp.roll(noise, 1, axis=1)
    rough = jnp.exp(jax.random.uniform(keys[1], (ROWS, 1), jnp.float32, math.log(0.7), math.log(1.4)))
    mixed = mixed * rough
    ramp = jnp.exp(math.log(3.0) * jnp.arange(ROWS, dtype=jnp.float32)[:, None] / jnp.float32(ROWS - 1))
    column = jnp.exp(jax.random.uniform(keys[2], (1, K), jnp.float32, math.log(0.3), math.log(3.0)))
    return jnp.clip(mixed * ramp * column, -120.0, 120.0).astype(jnp.float32)


def setup_inputs(seed: int = 0) -> dict:
    seeds = jax.random.split(jax.random.key(seed), 2)
    return {
        "sketch": draw_sketch(jax.random.fold_in(seeds[1], 71), 0),
    }


def reference(sketch):
    gram = lax.dot_general(sketch.astype(jnp.float32), sketch.astype(jnp.float32), (((0,), (0,)), ((), ())), precision=lax.Precision.HIGHEST, preferred_element_type=jnp.float32)
    eye = jnp.eye(K, dtype=jnp.float32)
    precision = eye + gram / jnp.float32(ROWS)
    inverse = jnp.linalg.solve(precision, eye)
    inverse = 0.5 * (inverse + inverse.T)
    posterior_basis = jnp.dot(sketch.astype(jnp.float32), inverse.astype(jnp.float32), precision=lax.Precision.HIGHEST, preferred_element_type=jnp.float32)
    logdet = jnp.linalg.slogdet(precision)[1]
    return (posterior_basis, (logdet / jnp.float32(K)).astype(jnp.float32))
```

```python
import functools

import jax
import jax.numpy as jnp
from jax import lax
from jax.experimental import pallas as pl
from jax.experimental.pallas import tpu as pltpu
from jax.sharding import PartitionSpec as P

AXES = ("crow", "ccol")
TILE = 128
F32 = jnp.float32
BF16 = jnp.bfloat16
LOG1P = {
    1: 0.9999739192217169,
    2: -0.49928683013429037,
    3: 0.32664225835205063,
    4: -0.21934280863425915,
    5: 0.12031934947180563,
    6: -0.037875575885947615,
    8: 0.0027171687390490683,
}
MAX_SQUARINGS = 12
VMEM_LIMIT = 48 * 1024 * 1024


def split(x):
    high = x.astype(BF16)
    return high, (x - high.astype(F32)).astype(BF16)


def split3(x):
    high = x.astype(BF16)
    rest = x - high.astype(F32)
    middle = rest.astype(BF16)
    return high, middle, (rest - middle.astype(F32)).astype(BF16)


def multiply(acc, left, staged=None):
    pltpu.matmul_acc_lhs(acc, left, load_staged_rhs=staged)


def sums_of(*units):
    for unit, terms in enumerate(units):
        for t, (tile, _) in enumerate(terms[:2]):
            pltpu.matmul_push_rhs(tile, t, unit)
    for t in range(max(len(terms) for terms in units)):
        for unit, terms in enumerate(units):
            if t < len(terms):
                for n, (acc, left) in enumerate(terms[t][1]):
                    multiply(acc, left, t % 2 if n == 0 else None)
                if t + 2 < len(terms):
                    pltpu.matmul_push_rhs(terms[t + 2][0], t % 2, unit)


def pop_both(one, two):
    return pltpu.matmul_pop(one) + pltpu.matmul_pop(two)


def dot6(accs, a, b):
    one, two = accs[:2]
    a0, a1, a2 = split3(a)
    b0, b1, b2 = split3(b)
    sums_of(
        [(b0, [(one, a0), (one, a1), (one, a2)])],
        [(b1, [(two, a0), (two, a1)]), (b2, [(two, a0)])],
    )
    return pop_both(one, two)


def eye_mask(n):
    return lax.broadcasted_iota(jnp.int32, (n, n), 0) == lax.broadcasted_iota(jnp.int32, (n, n), 1)


def above_mask(n):
    return lax.broadcasted_iota(jnp.int32, (n, n), 0) < lax.broadcasted_iota(jnp.int32, (n, n), 1)


class Plan:
    def __init__(self, nrow, ncol, width):
        self.ncol = ncol
        self.n = nrow * ncol
        self.parts = self.n // 4
        bits = [1 << b for b in range(1, self.n.bit_length() - 1)]
        y = [b for b in bits if b < ncol]
        x = [b for b in bits if ncol <= b < self.parts]
        self.z = [b for b in bits if b >= self.parts]
        self.stages = list(zip(x, y))
        tiles = width // TILE
        self.pairs = [(i, j) for i in range(tiles) for j in range(i + 1, tiles)]
        self.folds = [(i, i + 1) for i in range(0, tiles, 2)]
        self.diagonals = (len(self.pairs) + len(self.folds)) * TILE
        self.chunk = 8 * pl.cdiv(self.diagonals + 8, 8 * self.parts)
        self.half = self.chunk * self.parts // 2

    def me(self):
        return lax.axis_index("crow") * self.ncol + lax.axis_index("ccol")

    def rows(self, part, me):
        order = 0
        for mask in sum(self.stages, ()):
            here = jnp.bitwise_and(jnp.bitwise_xor(part, me), mask) // mask
            order = 2 * order + here
        return pl.ds(pl.multiple_of(order * self.chunk, 8), self.chunk)

    def halves(self, me, copy):
        for core in range(2):

            @pl.when(jnp.bitwise_and(me, 1) == core)
            def _():
                for part in range(self.parts):
                    copy(part, part & 1 == core)

    def swap(self, x, mask):
        return lax.ppermute(x, AXES, [(i, i ^ mask) for i in range(self.n)])


def gram_kernel(
    plan, sketch_ref, keep_ref, send_ref,
    rows_ref, flat, turned, whole, packed, load_sem,
):
    blocks = load_sem.shape[0]
    size = rows_ref.shape[0] // blocks
    width = rows_ref.shape[1]
    half = width // 2
    first, second = slice(0, half), slice(half, width)

    def load(i):
        at = pl.ds(i * size, size)
        return pltpu.make_async_copy(sketch_ref.at[at], rows_ref.at[at], load_sem.at[i])

    def prepare(i):
        load(i).wait()
        h, l = split(rows_ref[i * size : (i + 1) * size, :])
        flat[2 * (i % 2)] = h
        flat[2 * (i % 2) + 1] = l
        turned[2 * (i % 2)] = h.T
        turned[2 * (i % 2) + 1] = l.T

    def push(slot, staged):
        pltpu.matmul_push_rhs(flat[slot, :, first], staged, 0)
        pltpu.matmul_push_rhs(flat[slot, :, second], staged, 1)

    for i in range(blocks):
        load(i).start()
    prepare(0)

    def sums(s00, z10, c00, z01, s11, c11):
        push(0, 0)
        for i in range(blocks):
            h, l = 2 * (i % 2), 2 * (i % 2) + 1
            push(l, 1)
            multiply(s00, turned[h, first, :], 0)
            multiply(s11, turned[h, second, :], 0)
            multiply(z10, turned[h, second, :])
            if i + 1 < blocks:
                prepare(i + 1)
                push(2 * ((i + 1) % 2), 0)
            multiply(s00, turned[l, first, :], 1)
            multiply(z01, turned[l, first, :], 1)
            multiply(c00, turned[h, first, :])
            multiply(z01, turned[h, first, :])
            multiply(z10, turned[h, second, :])
            multiply(s11, turned[l, second, :])
            multiply(c11, turned[h, second, :])

        cross = pltpu.matmul_pop(c00)
        whole[first, first] = pltpu.matmul_pop(s00) + cross + cross.T
        whole[first, second] = pltpu.matmul_pop(z01) + pltpu.matmul_pop(z10).T
        cross = pltpu.matmul_pop(c11)
        whole[second, second] = pltpu.matmul_pop(s11) + cross + cross.T

    square = (half, half)
    units = (0, 0, 0, 1, 1, 1)
    pl.run_scoped(sums, *[pltpu.ACC(unit)(square, F32) for unit in units])
    tile = lambda i, j: whole[i * TILE : (i + 1) * TILE, j * TILE : (j + 1) * TILE]
    packed[plan.diagonals :, :] = jnp.zeros_like(packed[plan.diagonals :, :])
    for t, (i, j) in enumerate(plan.pairs):
        packed[t * TILE : (t + 1) * TILE, :] = tile(i, j)
    for f, (i, j) in enumerate(plan.folds):
        t = len(plan.pairs) + f
        packed[t * TILE : (t + 1) * TILE, :] = jnp.where(above_mask(TILE), tile(i, i), tile(j, j))
        line = jnp.sum(jnp.where(eye_mask(TILE), tile(i, i), 0.0), axis=0, keepdims=True)
        packed[plan.diagonals + f : plan.diagonals + f + 1, :] = line
    me = plan.me()

    def copy(part, own):
        ref = keep_ref if own else send_ref
        ref[plan.rows(part, me), :] = packed[part * plan.chunk : (part + 1) * plan.chunk, :]

    plan.halves(me, copy)


def gram(plan, sketch):
    rows, width = sketch.shape
    half = width // 2
    return pl.pallas_call(
        functools.partial(gram_kernel, plan),
        in_specs=[pl.BlockSpec(memory_space=pl.ANY)],
        out_specs=[pl.BlockSpec(memory_space=pltpu.VMEM)] * 2,
        out_shape=[jax.ShapeDtypeStruct((plan.half, TILE), F32)] * 2,
        scratch_shapes=[
            pltpu.VMEM((rows, width), F32),
            pltpu.VMEM((4, half, width), BF16),
            pltpu.VMEM((4, width, half), BF16),
            pltpu.VMEM((width, width), F32),
            pltpu.VMEM((2 * plan.half, TILE), F32),
            pltpu.SemaphoreType.DMA((rows // half,)),
        ],
        compiler_params=pltpu.CompilerParams(vmem_limit_bytes=VMEM_LIMIT),
    )(sketch)


def share(plan, keep, send):
    own = keep + plan.swap(send, 1)
    for x, y in plan.stages:
        m = own.shape[0] // 4
        got = [plan.swap(own[d * m : (d + 1) * m], k) for d, k in ((1, y), (2, x), (3, x + y))]
        own = own[:m] + got[0] + got[1] + got[2]
    for z in plan.z:
        own = own + plan.swap(own, z)
    for x, y in reversed(plan.stages):
        own = jnp.concatenate([own] + [plan.swap(own, k) for k in (y, x, x + y)], axis=0)
    return own, plan.swap(own, 1)


def fold(x):
    n = x.shape[0]
    return jnp.sum(x.reshape(n // 8, 8, x.shape[1]), axis=0)


def near_inverse(accs, a, o_ref, y_ref, acc_ref):
    n = a.shape[0]
    eye = eye_mask(n)
    diagonal = jnp.where(eye, a, 0.0)
    s_row = lax.rsqrt(jnp.sum(diagonal, axis=0, keepdims=True))
    s_col = lax.rsqrt(jnp.sum(diagonal, axis=1, keepdims=True))
    c = a * s_col * s_row
    norm = jnp.max(jnp.sum(jnp.abs(c), axis=0, keepdims=True), axis=1, keepdims=True)
    inv_norm = 1.0 / norm
    rho0 = 1.0 - inv_norm
    start = jnp.where(eye, 1.0 - rho0, 0.0) - c * inv_norm
    zero = jnp.zeros((n, n), F32)
    o_ref[0] = start
    o_ref[1] = zero
    o_ref[2] = zero
    y_ref[...] = zero
    acc_ref[...] = fold(jnp.where(eye, LOG1P[1] * (start + rho0), 0.0))
    square0, square1, factor0, factor1 = accs

    def more(carry):
        return jnp.logical_and(carry[0] < MAX_SQUARINGS, carry[1] >= 1e-3)

    def body(carry):
        k, _, rho, rho1, rho2, xi = carry
        o = o_ref[k % 3]
        y = y_ref[...]
        oh, ol = split(o)
        yh, yl = split(y)
        sums_of(
            [(oh, [(square0, oh), (square0, ol), (factor0, yh)])],
            [(oh, [(factor1, yl)]), (ol, [(square1, oh), (factor1, yh)])],
        )
        o1 = o_ref[(k + 2) % 3]
        o2 = o_ref[(k + 1) % 3]
        w0 = LOG1P[1] + LOG1P[2] + jnp.where(k >= 1, LOG1P[4], 0.0) + jnp.where(k >= 2, LOG1P[8], 0.0)
        w1 = jnp.where(k >= 1, LOG1P[3], 0.0) + jnp.where(k >= 2, LOG1P[6], 0.0)
        w2 = LOG1P[5]
        r = o + jnp.where(eye, rho, 0.0)
        mixed = w0 * o + w1 * o1 + w2 * o2 + jnp.where(eye, w0 * rho + w1 * rho1 + w2 * rho2, 0.0)
        acc_ref[...] += fold(r * mixed)
        size = jnp.sum(fold(r * r))
        o_ref[(k + 1) % 3] = (2.0 * rho) * o + pop_both(square0, square1)
        y_ref[...] = (1.0 + rho) * y + xi * o + pop_both(factor0, factor1)
        return k + 1, size, rho * rho, rho, rho1, xi * (1.0 + rho)

    none = jnp.float32(0.0)
    begin = (jnp.int32(0), jnp.float32(1e30), jnp.max(rho0), none, none, jnp.max(inv_norm))
    _, size, _, _, _, xi = lax.while_loop(more, body, begin)
    x = y_ref[...] + jnp.where(eye, xi, 0.0)
    rest = jnp.where(eye, 1.0, 0.0) - dot6(accs, c, x)
    sums_of([(rest.astype(BF16), [(square0, x.astype(BF16))])])
    x = x + pltpu.matmul_pop(square0)
    log_det = n * jnp.log(norm) - jnp.sum(acc_ref[...], keepdims=True) - 2.0 * jnp.sum(
        jnp.log(s_row), axis=1, keepdims=True
    )
    return x * s_col * s_row, log_det, size


def sweep(a_ref, c_ref, log_ref):
    n = a_ref.shape[0]
    eye = eye_mask(n)
    diagonal = jnp.where(eye, a_ref[...], 0.0)
    s_row = lax.rsqrt(jnp.sum(diagonal, axis=0, keepdims=True))
    s_col = lax.rsqrt(jnp.sum(diagonal, axis=1, keepdims=True))
    c_ref[...] = a_ref[...] * s_col * s_row
    log_ref[...] = -2.0 * jnp.sum(jnp.log(s_row), axis=1, keepdims=True)
    lane = lax.broadcasted_iota(jnp.int32, (1, n), 1)

    @pl.loop(0, n)
    def _(k):
        row = c_ref[pl.ds(k, 1), :]
        here = lane == k
        pivot = jnp.sum(jnp.where(here, row, 0.0), axis=1, keepdims=True)
        log_ref[...] += jnp.log(pivot)
        u = jnp.where(here, pivot - 1.0, row)
        column = jnp.broadcast_to(u, (8, n)).T[:, :1]
        outer = column * (u / pivot)
        c_ref[...] = c_ref[...] - outer
        c_ref[pl.ds(k, 1), :] = c_ref[pl.ds(k, 1), :] - jnp.where(here, 2.0, 0.0)

    c_ref[...] = -(c_ref[...] * s_col * s_row)


def solve_kernel(
    plan, rows_all, near_ref, far_ref, sketch_ref, out_ref, log_ref,
    packed, a_ref, x_ref, o_ref, y_ref, acc_ref,
    rows_ref, result, mats, parts, load_sem, store_sem,
):
    blocks = load_sem.shape[0]
    size = rows_ref.shape[0] // blocks

    def load(i):
        at = pl.ds(i * size, size)
        return pltpu.make_async_copy(sketch_ref.at[at], rows_ref.at[at], load_sem.at[i])

    def store(i):
        at = pl.ds(i * size, size)
        return pltpu.make_async_copy(result.at[at], out_ref.at[at], store_sem.at[i])

    for i in range(blocks):
        load(i).start()

    n = a_ref.shape[0]
    m = n // 2
    me = plan.me()

    def copy(part, own):
        ref = near_ref if own else far_ref
        packed[part * plan.chunk : (part + 1) * plan.chunk, :] = ref[plan.rows(part, me), :]

    plan.halves(me, copy)

    scale = jnp.float32(1.0 / rows_all)
    unit = jnp.where(eye_mask(TILE), 1.0, 0.0)
    rows = lambda i: slice(i * TILE, (i + 1) * TILE)
    for t, (i, j) in enumerate(plan.pairs):
        tile = packed[rows(t), :] * scale
        a_ref[rows(i), rows(j)] = tile
        a_ref[rows(j), rows(i)] = tile.T
    above = above_mask(TILE)
    for f, (i, j) in enumerate(plan.folds):
        tile = packed[rows(len(plan.pairs) + f), :] * scale
        line = packed[plan.diagonals + f : plan.diagonals + f + 1, :] * scale
        mixed = jnp.where(eye_mask(TILE), line, jnp.where(above, tile, tile.T))
        a_ref[rows(i), rows(i)] = mixed + unit
        a_ref[rows(j), rows(j)] = jnp.where(above, tile.T, tile) + unit

    bufs = (o_ref, y_ref, acc_ref)

    def invert(*accs):
        x11, log1, size1 = near_inverse(accs, a_ref[:m, :m], *bufs)
        t12 = dot6(accs, x11, a_ref[:m, m:])
        schur = a_ref[m:, m:] - dot6(accs, a_ref[m:, :m], t12)
        x_ref[:m, :m] = x11
        x_ref[:m, m:] = t12
        x22, log2, size2 = near_inverse(accs, schur, *bufs)
        t12 = x_ref[:m, m:]
        x12 = -dot6(accs, t12, x22)
        x_ref[:m, :m] = x_ref[:m, :m] - dot6(accs, x12, t12.T)
        x_ref[:m, m:] = x12
        x_ref[m:, :m] = x12.T
        x_ref[m:, m:] = x22
        log_ref[...] = log1 + log2
        good = jnp.logical_and(size1 < 1e-3, size2 < 1e-3)

        @pl.when(jnp.logical_not(good))
        def _():
            sweep(a_ref, x_ref, log_ref)

    pl.run_scoped(invert, *[pltpu.ACC(unit)((m, m), F32) for unit in (0, 1, 0, 1)])
    log_ref[...] = log_ref[...] / n
    eye = eye_mask(n)
    diagonal = jnp.sum(jnp.where(eye, x_ref[...], 0.0), axis=0, keepdims=True)
    high, low = split(jnp.where(eye, 0.0, x_ref[...]))
    mats[0] = high
    mats[1] = low
    for i in range(blocks):
        load(i).wait()

    def prepare(i):
        h, l = split(rows_ref[i * size : (i + 1) * size, :])
        parts[2 * (i % 2)] = h
        parts[2 * (i % 2) + 1] = l

    steps = [(i, k, which) for i in range(blocks) for k in range(2) for which in range(2)]

    def push(step):
        _, k, which = steps[step]
        for unit in range(2):
            tile = mats[which, k * m : (k + 1) * m, unit * m : (unit + 1) * m]
            pltpu.matmul_push_rhs(tile, which, unit)

    def products(*accs):
        push(0)
        push(1)
        prepare(0)
        for step, (i, k, which) in enumerate(steps):
            h, l = 2 * (i % 2), 2 * (i % 2) + 1
            mine = accs[h : h + 2]
            cols = slice(k * m, (k + 1) * m)
            for acc in mine:
                multiply(acc, parts[h, :, cols], which)
            if which == 0:
                for acc in mine:
                    multiply(acc, parts[l, :, cols])
            if step + 2 < len(steps):
                push(step + 2)
            if k == 0 and which == 1 and i + 1 < blocks:
                prepare(i + 1)
            if k == 1 and which == 1:
                at = slice(i * size, (i + 1) * size)
                for unit, acc in enumerate(mine):
                    cols = slice(unit * m, (unit + 1) * m)
                    result[at, cols] = rows_ref[at, cols] * diagonal[:, cols] + pltpu.matmul_pop(acc)
                store(i).start()

    pl.run_scoped(products, *[pltpu.ACC(unit)((size, m), F32) for unit in (0, 1, 0, 1)])
    for i in range(blocks):
        store(i).wait()


def solve(plan, sketch, near, far):
    rows, width = sketch.shape
    m = width // 2
    block = min(512, rows)
    vmem = pl.BlockSpec(memory_space=pltpu.VMEM)
    hbm = pl.BlockSpec(memory_space=pl.ANY)
    return pl.pallas_call(
        functools.partial(solve_kernel, plan, rows * plan.n),
        in_specs=[vmem, vmem, hbm],
        out_specs=[hbm, vmem],
        out_shape=[
            jax.ShapeDtypeStruct((rows, width), F32),
            jax.ShapeDtypeStruct((1, 1), F32),
        ],
        scratch_shapes=[
            pltpu.VMEM((2 * plan.half, TILE), F32),
            pltpu.VMEM((width, width), F32),
            pltpu.VMEM((width, width), F32),
            pltpu.VMEM((3, m, m), F32),
            pltpu.VMEM((m, m), F32),
            pltpu.VMEM((8, m), F32),
            pltpu.VMEM((rows, width), F32),
            pltpu.VMEM((rows, width), F32),
            pltpu.VMEM((2, width, width), BF16),
            pltpu.VMEM((4, block, width), BF16),
            pltpu.SemaphoreType.DMA((rows // block,)),
            pltpu.SemaphoreType.DMA((rows // block,)),
        ],
        compiler_params=pltpu.CompilerParams(vmem_limit_bytes=VMEM_LIMIT),
    )(near, far, sketch)


def solution(mesh):
    nrow, ncol = mesh.shape["crow"], mesh.shape["ccol"]

    def on_device(sketch):
        plan = Plan(nrow, ncol, sketch.shape[1])
        keep, send = gram(plan, sketch)
        near, far = share(plan, keep, send)
        basis, log_mean = solve(plan, sketch, near, far)
        return basis, log_mean[0, 0]

    return jax.shard_map(
        on_device,
        mesh=mesh,
        in_specs=(P(AXES, None),),
        out_specs=(P(AXES, None), P()),
        check_vma=False,
    )
```

```python
import functools

import jax
import jax.numpy as jnp
from jax import lax
from jax.experimental import pallas as pl
from jax.experimental.pallas import tpu as pltpu
from jax.sharding import PartitionSpec as P

AXES = ("crow", "ccol")
TILE = 128
F32 = jnp.float32
BF16 = jnp.bfloat16
LOG1P = {
    1: 0.9999739192217169,
    2: -0.49928683013429037,
    3: 0.32664225835205063,
    4: -0.21934280863425915,
    5: 0.12031934947180563,
    6: -0.037875575885947615,
    8: 0.0027171687390490683,
}
MAX_SQUARINGS = 12
VMEM_LIMIT = 48 * 1024 * 1024


def split(x):
    high = x.astype(BF16)
    return high, (x - high.astype(F32)).astype(BF16)


def split3(x):
    high = x.astype(BF16)
    rest = x - high.astype(F32)
    middle = rest.astype(BF16)
    return high, middle, (rest - middle.astype(F32)).astype(BF16)


def multiply(acc, left, staged=None):
    pltpu.matmul_acc_lhs(acc, left, load_staged_rhs=staged)


def sums_of(*units):
    for unit, terms in enumerate(units):
        for t, (tile, _) in enumerate(terms[:2]):
            pltpu.matmul_push_rhs(tile, t, unit)
    for t in range(max(len(terms) for terms in units)):
        for unit, terms in enumerate(units):
            if t < len(terms):
                for n, (acc, left) in enumerate(terms[t][1]):
                    multiply(acc, left, t % 2 if n == 0 else None)
                if t + 2 < len(terms):
                    pltpu.matmul_push_rhs(terms[t + 2][0], t % 2, unit)


def pop_both(one, two):
    return pltpu.matmul_pop(one) + pltpu.matmul_pop(two)


def dot6(accs, a, b):
    one, two = accs[:2]
    a0, a1, a2 = split3(a)
    b0, b1, b2 = split3(b)
    sums_of(
        [(b0, [(one, a0), (one, a1), (one, a2)])],
        [(b1, [(two, a0), (two, a1)]), (b2, [(two, a0)])],
    )
    return pop_both(one, two)


def eye_mask(n):
    return lax.broadcasted_iota(jnp.int32, (n, n), 0) == lax.broadcasted_iota(jnp.int32, (n, n), 1)


def above_mask(n):
    return lax.broadcasted_iota(jnp.int32, (n, n), 0) < lax.broadcasted_iota(jnp.int32, (n, n), 1)


class Plan:
    def __init__(self, nrow, ncol, width):
        self.ncol = ncol
        self.n = nrow * ncol
        self.parts = self.n // 4
        bits = [1 << b for b in range(1, self.n.bit_length() - 1)]
        y = [b for b in bits if b < ncol]
        x = [b for b in bits if ncol <= b < self.parts]
        self.z = [b for b in bits if b >= self.parts]
        self.stages = list(zip(x, y))
        tiles = width // TILE
        self.pairs = [(i, j) for i in range(tiles) for j in range(i + 1, tiles)]
        self.folds = [(i, i + 1) for i in range(0, tiles, 2)]
        self.diagonals = (len(self.pairs) + len(self.folds)) * TILE
        self.chunk = 8 * pl.cdiv(self.diagonals + 8, 8 * self.parts)
        self.half = self.chunk * self.parts // 2

    def me(self):
        return lax.axis_index("crow") * self.ncol + lax.axis_index("ccol")

    def rows(self, part, me):
        order = 0
        for mask in sum(self.stages, ()):
            here = jnp.bitwise_and(jnp.bitwise_xor(part, me), mask) // mask
            order = 2 * order + here
        return pl.ds(pl.multiple_of(order * self.chunk, 8), self.chunk)

    def halves(self, me, copy):
        for core in range(2):

            @pl.when(jnp.bitwise_and(me, 1) == core)
            def _():
                for part in range(self.parts):
                    copy(part, part & 1 == core)

    def swap(self, x, mask):
        return lax.ppermute(x, AXES, [(i, i ^ mask) for i in range(self.n)])


def gram_kernel(
    plan, sketch_ref, keep_ref, send_ref,
    rows_ref, flat, turned, whole, packed, load_sem,
):
    blocks = load_sem.shape[0]
    size = rows_ref.shape[0] // blocks
    width = rows_ref.shape[1]
    half = width // 2
    first, second = slice(0, half), slice(half, width)

    def load(i):
        at = pl.ds(i * size, size)
        return pltpu.make_async_copy(sketch_ref.at[at], rows_ref.at[at], load_sem.at[i])

    def prepare(i):
        load(i).wait()
        h, l = split(rows_ref[i * size : (i + 1) * size, :])
        flat[2 * (i % 2)] = h
        flat[2 * (i % 2) + 1] = l
        turned[2 * (i % 2)] = h.T
        turned[2 * (i % 2) + 1] = l.T

    def push(slot, staged):
        pltpu.matmul_push_rhs(flat[slot, :, first], staged, 0)
        pltpu.matmul_push_rhs(flat[slot, :, second], staged, 1)

    for i in range(blocks):
        load(i).start()
    prepare(0)

    def sums(s00, z10, c00, z01, s11, c11):
        push(0, 0)
        for i in range(blocks):
            h, l = 2 * (i % 2), 2 * (i % 2) + 1
            push(l, 1)
            multiply(s00, turned[h, first, :], 0)
            multiply(s11, turned[h, second, :], 0)
            multiply(z10, turned[h, second, :])
            if i + 1 < blocks:
                prepare(i + 1)
                push(2 * ((i + 1) % 2), 0)
            multiply(s00, turned[l, first, :], 1)
            multiply(z01, turned[l, first, :], 1)
            multiply(c00, turned[h, first, :])
            multiply(z01, turned[h, first, :])
            multiply(z10, turned[h, second, :])
            multiply(s11, turned[l, second, :])
            multiply(c11, turned[h, second, :])

        cross = pltpu.matmul_pop(c00)
        whole[first, first] = pltpu.matmul_pop(s00) + cross + cross.T
        whole[first, second] = pltpu.matmul_pop(z01) + pltpu.matmul_pop(z10).T
        cross = pltpu.matmul_pop(c11)
        whole[second, second] = pltpu.matmul_pop(s11) + cross + cross.T

    square = (half, half)
    units = (0, 0, 0, 1, 1, 1)
    pl.run_scoped(sums, *[pltpu.ACC(unit)(square, F32) for unit in units])
    tile = lambda i, j: whole[i * TILE : (i + 1) * TILE, j * TILE : (j + 1) * TILE]
    packed[plan.diagonals :, :] = jnp.zeros_like(packed[plan.diagonals :, :])
    for t, (i, j) in enumerate(plan.pairs):
        packed[t * TILE : (t + 1) * TILE, :] = tile(i, j)
    for f, (i, j) in enumerate(plan.folds):
        t = len(plan.pairs) + f
        packed[t * TILE : (t + 1) * TILE, :] = jnp.where(above_mask(TILE), tile(i, i), tile(j, j))
        line = jnp.sum(jnp.where(eye_mask(TILE), tile(i, i), 0.0), axis=0, keepdims=True)
        packed[plan.diagonals + f : plan.diagonals + f + 1, :] = line
    me = plan.me()

    def copy(part, own):
        ref = keep_ref if own else send_ref
        ref[plan.rows(part, me), :] = packed[part * plan.chunk : (part + 1) * plan.chunk, :]

    plan.halves(me, copy)


def gram(plan, sketch):
    rows, width = sketch.shape
    half = width // 2
    return pl.pallas_call(
        functools.partial(gram_kernel, plan),
        in_specs=[pl.BlockSpec(memory_space=pl.ANY)],
        out_specs=[pl.BlockSpec(memory_space=pltpu.VMEM)] * 2,
        out_shape=[jax.ShapeDtypeStruct((plan.half, TILE), F32)] * 2,
        scratch_shapes=[
            pltpu.VMEM((rows, width), F32),
            pltpu.VMEM((4, half, width), BF16),
            pltpu.VMEM((4, width, half), BF16),
            pltpu.VMEM((width, width), F32),
            pltpu.VMEM((2 * plan.half, TILE), F32),
            pltpu.SemaphoreType.DMA((rows // half,)),
        ],
        compiler_params=pltpu.CompilerParams(vmem_limit_bytes=VMEM_LIMIT),
    )(sketch)


def share(plan, keep, send):
    own = keep + plan.swap(send, 1)
    for x, y in plan.stages:
        m = own.shape[0] // 4
        got = [plan.swap(own[d * m : (d + 1) * m], k) for d, k in ((1, y), (2, x), (3, x + y))]
        own = own[:m] + got[0] + got[1] + got[2]
    one, two = plan.z
    got = [plan.swap(own, z) for z in (one, two, one + two)]
    own = (own + got[0]) + (got[1] + got[2])
    for x, y in reversed(plan.stages):
        own = jnp.concatenate([own] + [plan.swap(own, k) for k in (y, x, x + y)], axis=0)
    return own, plan.swap(own, 1)


def fold(x):
    n = x.shape[0]
    return jnp.sum(x.reshape(n // 8, 8, x.shape[1]), axis=0)


def near_inverse(accs, a, o_ref, y_ref, r1_ref, r2_ref, acc_ref):
    n = a.shape[0]
    eye = eye_mask(n)
    diagonal = jnp.where(eye, a, 0.0)
    s_row = lax.rsqrt(jnp.sum(diagonal, axis=0, keepdims=True))
    s_col = lax.rsqrt(jnp.sum(diagonal, axis=1, keepdims=True))
    c = a * s_col * s_row
    norm = jnp.max(jnp.sum(jnp.abs(c), axis=0, keepdims=True), axis=1, keepdims=True)
    inv_norm = 1.0 / norm
    rho0 = 1.0 - inv_norm
    start = jnp.where(eye, 1.0 - rho0, 0.0) - c * inv_norm
    o_ref[...] = start
    for ref in (y_ref, r1_ref, r2_ref):
        ref[...] = jnp.zeros((n, n), F32)
    acc_ref[...] = fold(jnp.where(eye, LOG1P[1] * (start + rho0), 0.0))
    square0, square1, factor0, factor1 = accs

    def more(carry):
        return jnp.logical_and(carry[0] < MAX_SQUARINGS, carry[1] >= 1e-3)

    def body(carry):
        k, _, rho, xi = carry
        o = o_ref[...]
        y = y_ref[...]
        oh, ol = split(o)
        yh, yl = split(y)
        sums_of(
            [(oh, [(square0, oh), (square0, ol), (factor0, yh)])],
            [(ol, [(square1, oh), (factor1, yh)]), (oh, [(factor1, yl)])],
        )
        r1 = r1_ref[...]
        r = o + jnp.where(eye, rho, 0.0)
        w0 = LOG1P[1] + LOG1P[2] + jnp.where(k >= 1, LOG1P[4], 0.0) + jnp.where(k >= 2, LOG1P[8], 0.0)
        w1 = jnp.where(k >= 1, LOG1P[3], 0.0) + jnp.where(k >= 2, LOG1P[6], 0.0)
        acc_ref[...] += fold(r * (w0 * r + w1 * r1 + LOG1P[5] * r2_ref[...]))
        size = jnp.sum(fold(r * r))
        r2_ref[...] = r1
        r1_ref[...] = r
        o_ref[...] = (2.0 * rho) * o + pop_both(square0, square1)
        y_ref[...] = (1.0 + rho) * y + xi * o + pop_both(factor0, factor1)
        return k + 1, size, rho * rho, xi * (1.0 + rho)

    begin = (jnp.int32(0), jnp.float32(1e30), jnp.max(rho0), jnp.max(inv_norm))
    _, size, _, xi = lax.while_loop(more, body, begin)
    x = y_ref[...] + jnp.where(eye, xi, 0.0)
    rest = jnp.where(eye, 1.0, 0.0) - dot6(accs, c, x)
    sums_of([(rest.astype(BF16), [(square0, x.astype(BF16))])])
    x = x + pltpu.matmul_pop(square0)
    log_det = n * jnp.log(norm) - jnp.sum(acc_ref[...], keepdims=True) - 2.0 * jnp.sum(
        jnp.log(s_row), axis=1, keepdims=True
    )
    return x * s_col * s_row, log_det, size


def sweep(a_ref, c_ref, log_ref):
    n = a_ref.shape[0]
    eye = eye_mask(n)
    diagonal = jnp.where(eye, a_ref[...], 0.0)
    s_row = lax.rsqrt(jnp.sum(diagonal, axis=0, keepdims=True))
    s_col = lax.rsqrt(jnp.sum(diagonal, axis=1, keepdims=True))
    c_ref[...] = a_ref[...] * s_col * s_row
    log_ref[...] = -2.0 * jnp.sum(jnp.log(s_row), axis=1, keepdims=True)
    lane = lax.broadcasted_iota(jnp.int32, (1, n), 1)

    @pl.loop(0, n)
    def _(k):
        row = c_ref[pl.ds(k, 1), :]
        here = lane == k
        pivot = jnp.sum(jnp.where(here, row, 0.0), axis=1, keepdims=True)
        log_ref[...] += jnp.log(pivot)
        u = jnp.where(here, pivot - 1.0, row)
        column = jnp.broadcast_to(u, (8, n)).T[:, :1]
        outer = column * (u / pivot)
        c_ref[...] = c_ref[...] - outer
        c_ref[pl.ds(k, 1), :] = c_ref[pl.ds(k, 1), :] - jnp.where(here, 2.0, 0.0)

    c_ref[...] = -(c_ref[...] * s_col * s_row)


def solve_kernel(
    plan, rows_all, near_ref, far_ref, sketch_ref, out_ref, log_ref,
    packed, a_ref, x_ref, o_ref, y_ref, r1_ref, r2_ref, acc_ref,
    rows_ref, result, mats, parts, load_sem, store_sem,
):
    blocks = load_sem.shape[0]
    size = rows_ref.shape[0] // blocks

    def load(i):
        at = pl.ds(i * size, size)
        return pltpu.make_async_copy(sketch_ref.at[at], rows_ref.at[at], load_sem.at[i])

    def store(i):
        at = pl.ds(i * size, size)
        return pltpu.make_async_copy(result.at[at], out_ref.at[at], store_sem.at[i])

    for i in range(blocks):
        load(i).start()

    n = a_ref.shape[0]
    m = n // 2
    me = plan.me()

    def copy(part, own):
        ref = near_ref if own else far_ref
        packed[part * plan.chunk : (part + 1) * plan.chunk, :] = ref[plan.rows(part, me), :]

    plan.halves(me, copy)

    scale = jnp.float32(1.0 / rows_all)
    unit = jnp.where(eye_mask(TILE), 1.0, 0.0)
    rows = lambda i: slice(i * TILE, (i + 1) * TILE)
    for t, (i, j) in enumerate(plan.pairs):
        tile = packed[rows(t), :] * scale
        a_ref[rows(i), rows(j)] = tile
        a_ref[rows(j), rows(i)] = tile.T
    above = above_mask(TILE)
    for f, (i, j) in enumerate(plan.folds):
        tile = packed[rows(len(plan.pairs) + f), :] * scale
        line = packed[plan.diagonals + f : plan.diagonals + f + 1, :] * scale
        mixed = jnp.where(eye_mask(TILE), line, jnp.where(above, tile, tile.T))
        a_ref[rows(i), rows(i)] = mixed + unit
        a_ref[rows(j), rows(j)] = jnp.where(above, tile.T, tile) + unit

    bufs = (o_ref, y_ref, r1_ref, r2_ref, acc_ref)

    def invert(*accs):
        x11, log1, size1 = near_inverse(accs, a_ref[:m, :m], *bufs)
        t12 = dot6(accs, x11, a_ref[:m, m:])
        schur = a_ref[m:, m:] - dot6(accs, a_ref[m:, :m], t12)
        x_ref[:m, :m] = x11
        x_ref[:m, m:] = t12
        x22, log2, size2 = near_inverse(accs, schur, *bufs)
        t12 = x_ref[:m, m:]
        x12 = -dot6(accs, t12, x22)
        x_ref[:m, :m] = x_ref[:m, :m] - dot6(accs, x12, t12.T)
        x_ref[:m, m:] = x12
        x_ref[m:, :m] = x12.T
        x_ref[m:, m:] = x22
        log_ref[...] = log1 + log2
        good = jnp.logical_and(size1 < 1e-3, size2 < 1e-3)

        @pl.when(jnp.logical_not(good))
        def _():
            sweep(a_ref, x_ref, log_ref)

    pl.run_scoped(invert, *[pltpu.ACC(unit)((m, m), F32) for unit in (0, 1, 0, 1)])
    log_ref[...] = log_ref[...] / n
    eye = eye_mask(n)
    diagonal = jnp.sum(jnp.where(eye, x_ref[...], 0.0), axis=0, keepdims=True)
    high, low = split(jnp.where(eye, 0.0, x_ref[...]))
    mats[0] = high
    mats[1] = low
    for i in range(blocks):
        load(i).wait()

    def prepare(i):
        h, l = split(rows_ref[i * size : (i + 1) * size, :])
        parts[2 * (i % 2)] = h
        parts[2 * (i % 2) + 1] = l

    steps = [(i, k, which) for i in range(blocks) for k in range(2) for which in range(2)]

    def push(step):
        _, k, which = steps[step]
        for unit in range(2):
            tile = mats[which, k * m : (k + 1) * m, unit * m : (unit + 1) * m]
            pltpu.matmul_push_rhs(tile, which, unit)

    def products(*accs):
        push(0)
        push(1)
        prepare(0)
        for step, (i, k, which) in enumerate(steps):
            h, l = 2 * (i % 2), 2 * (i % 2) + 1
            mine = accs[h : h + 2]
            cols = slice(k * m, (k + 1) * m)
            for acc in mine:
                multiply(acc, parts[h, :, cols], which)
            if which == 0:
                for acc in mine:
                    multiply(acc, parts[l, :, cols])
            if step + 2 < len(steps):
                push(step + 2)
            if k == 0 and which == 1 and i + 1 < blocks:
                prepare(i + 1)
            if k == 1 and which == 1:
                at = slice(i * size, (i + 1) * size)
                for unit, acc in enumerate(mine):
                    cols = slice(unit * m, (unit + 1) * m)
                    result[at, cols] = rows_ref[at, cols] * diagonal[:, cols] + pltpu.matmul_pop(acc)
                store(i).start()

    pl.run_scoped(products, *[pltpu.ACC(unit)((size, m), F32) for unit in (0, 1, 0, 1)])
    for i in range(blocks):
        store(i).wait()


def solve(plan, sketch, near, far):
    rows, width = sketch.shape
    m = width // 2
    block = min(512, rows)
    vmem = pl.BlockSpec(memory_space=pltpu.VMEM)
    hbm = pl.BlockSpec(memory_space=pl.ANY)
    return pl.pallas_call(
        functools.partial(solve_kernel, plan, rows * plan.n),
        in_specs=[vmem, vmem, hbm],
        out_specs=[hbm, vmem],
        out_shape=[
            jax.ShapeDtypeStruct((rows, width), F32),
            jax.ShapeDtypeStruct((1, 1), F32),
        ],
        scratch_shapes=[
            pltpu.VMEM((2 * plan.half, TILE), F32),
            pltpu.VMEM((width, width), F32),
            pltpu.VMEM((width, width), F32),
            pltpu.VMEM((m, m), F32),
            pltpu.VMEM((m, m), F32),
            pltpu.VMEM((m, m), F32),
            pltpu.VMEM((m, m), F32),
            pltpu.VMEM((8, m), F32),
            pltpu.VMEM((rows, width), F32),
            pltpu.VMEM((rows, width), F32),
            pltpu.VMEM((2, width, width), BF16),
            pltpu.VMEM((4, block, width), BF16),
            pltpu.SemaphoreType.DMA((rows // block,)),
            pltpu.SemaphoreType.DMA((rows // block,)),
        ],
        compiler_params=pltpu.CompilerParams(vmem_limit_bytes=VMEM_LIMIT),
    )(near, far, sketch)


def solution(mesh):
    nrow, ncol = mesh.shape["crow"], mesh.shape["ccol"]

    def on_device(sketch):
        plan = Plan(nrow, ncol, sketch.shape[1])
        keep, send = gram(plan, sketch)
        near, far = share(plan, keep, send)
        basis, log_mean = solve(plan, sketch, near, far)
        return basis, log_mean[0, 0]

    return jax.shard_map(
        on_device,
        mesh=mesh,
        in_specs=(P(AXES, None),),
        out_specs=(P(AXES, None), P()),
        check_vma=False,
    )
```

```python
import functools

import jax
import jax.numpy as jnp
from jax import lax
from jax.experimental import pallas as pl
from jax.experimental.pallas import tpu as pltpu
from jax.sharding import PartitionSpec as P

AXES = ("crow", "ccol")
TILE = 128
F32 = jnp.float32
BF16 = jnp.bfloat16
LOG1P = {
    1: 0.9999739192217169,
    2: -0.49928683013429037,
    3: 0.32664225835205063,
    4: -0.21934280863425915,
    5: 0.12031934947180563,
    6: -0.037875575885947615,
    8: 0.0027171687390490683,
}
MAX_SQUARINGS = 12
VMEM_LIMIT = 48 * 1024 * 1024


def split(x):
    high = x.astype(BF16)
    return high, (x - high.astype(F32)).astype(BF16)


def split3(x):
    high = x.astype(BF16)
    rest = x - high.astype(F32)
    middle = rest.astype(BF16)
    return high, middle, (rest - middle.astype(F32)).astype(BF16)


def multiply(acc, left, staged=None):
    pltpu.matmul_acc_lhs(acc, left, load_staged_rhs=staged)


def sums_of(*units):
    for unit, terms in enumerate(units):
        for t, (tile, _) in enumerate(terms[:2]):
            pltpu.matmul_push_rhs(tile, t, unit)
    for t in range(max(len(terms) for terms in units)):
        for unit, terms in enumerate(units):
            if t < len(terms):
                for n, (acc, left) in enumerate(terms[t][1]):
                    multiply(acc, left, t % 2 if n == 0 else None)
                if t + 2 < len(terms):
                    pltpu.matmul_push_rhs(terms[t + 2][0], t % 2, unit)


def pop_both(one, two):
    return pltpu.matmul_pop(one) + pltpu.matmul_pop(two)


def dot6(accs, a, b):
    one, two = accs[:2]
    a0, a1, a2 = split3(a)
    b0, b1, b2 = split3(b)
    sums_of(
        [(b0, [(one, a0), (one, a1), (one, a2)])],
        [(b1, [(two, a0), (two, a1)]), (b2, [(two, a0)])],
    )
    return pop_both(one, two)


def eye_mask(n):
    return lax.broadcasted_iota(jnp.int32, (n, n), 0) == lax.broadcasted_iota(jnp.int32, (n, n), 1)


def above_mask(n):
    return lax.broadcasted_iota(jnp.int32, (n, n), 0) < lax.broadcasted_iota(jnp.int32, (n, n), 1)


class Plan:
    def __init__(self, nrow, ncol, width):
        self.ncol = ncol
        self.n = nrow * ncol
        self.parts = self.n // 4
        bits = [1 << b for b in range(1, self.n.bit_length() - 1)]
        y = [b for b in bits if b < ncol]
        x = [b for b in bits if ncol <= b < self.parts]
        self.z = [b for b in bits if b >= self.parts]
        self.stages = list(zip(x, y))
        tiles = width // TILE
        self.pairs = [(i, j) for i in range(tiles) for j in range(i + 1, tiles)]
        self.folds = [(i, i + 1) for i in range(0, tiles, 2)]
        self.diagonals = (len(self.pairs) + len(self.folds)) * TILE
        self.chunk = 8 * pl.cdiv(self.diagonals + 8, 8 * self.parts)
        self.half = self.chunk * self.parts // 2

    def me(self):
        return lax.axis_index("crow") * self.ncol + lax.axis_index("ccol")

    def rows(self, part, me):
        order = 0
        for mask in sum(self.stages, ()):
            here = jnp.bitwise_and(jnp.bitwise_xor(part, me), mask) // mask
            order = 2 * order + here
        return pl.ds(pl.multiple_of(order * self.chunk, 8), self.chunk)

    def halves(self, me, copy):
        for core in range(2):

            @pl.when(jnp.bitwise_and(me, 1) == core)
            def _():
                for part in range(self.parts):
                    copy(part, part & 1 == core)

    def swap(self, x, mask):
        return lax.ppermute(x, AXES, [(i, i ^ mask) for i in range(self.n)])


def gram_kernel(
    plan, sketch_ref, keep_ref, send_ref,
    rows_ref, flat, turned, whole, packed, load_sem,
):
    blocks = load_sem.shape[0]
    size = rows_ref.shape[0] // blocks
    width = rows_ref.shape[1]
    half = width // 2
    first, second = slice(0, half), slice(half, width)

    def load(i):
        at = pl.ds(i * size, size)
        return pltpu.make_async_copy(sketch_ref.at[at], rows_ref.at[at], load_sem.at[i])

    def prepare(i):
        if i != 1 and i & (i - 1) == 0:
            for j in range(i, min(max(2 * i, 2), blocks)):
                load(j).wait()
        h, l = split(rows_ref[i * size : (i + 1) * size, :])
        flat[2 * (i % 2)] = h
        flat[2 * (i % 2) + 1] = l
        turned[2 * (i % 2)] = h.T
        turned[2 * (i % 2) + 1] = l.T

    def push(slot, staged):
        pltpu.matmul_push_rhs(flat[slot, :, first], staged, 0)
        pltpu.matmul_push_rhs(flat[slot, :, second], staged, 1)

    for i in range(blocks):
        load(i).start()
    prepare(0)

    def sums(s00, z10, c00, z01, s11, c11):
        push(0, 0)
        for i in range(blocks):
            h, l = 2 * (i % 2), 2 * (i % 2) + 1
            push(l, 1)
            multiply(s00, turned[h, first, :], 0)
            multiply(s11, turned[h, second, :], 0)
            multiply(z10, turned[h, second, :])
            if i + 1 < blocks:
                prepare(i + 1)
                push(2 * ((i + 1) % 2), 0)
            multiply(s00, turned[l, first, :], 1)
            multiply(z01, turned[l, first, :], 1)
            multiply(c00, turned[h, first, :])
            multiply(z01, turned[h, first, :])
            multiply(z10, turned[h, second, :])
            multiply(s11, turned[l, second, :])
            multiply(c11, turned[h, second, :])

        cross = pltpu.matmul_pop(c00)
        whole[first, first] = pltpu.matmul_pop(s00) + cross + cross.T
        whole[first, second] = pltpu.matmul_pop(z01) + pltpu.matmul_pop(z10).T
        cross = pltpu.matmul_pop(c11)
        whole[second, second] = pltpu.matmul_pop(s11) + cross + cross.T

    square = (half, half)
    units = (0, 0, 0, 1, 1, 1)
    pl.run_scoped(sums, *[pltpu.ACC(unit)(square, F32) for unit in units])
    tile = lambda i, j: whole[i * TILE : (i + 1) * TILE, j * TILE : (j + 1) * TILE]
    packed[plan.diagonals :, :] = jnp.zeros_like(packed[plan.diagonals :, :])
    for t, (i, j) in enumerate(plan.pairs):
        packed[t * TILE : (t + 1) * TILE, :] = tile(i, j)
    for f, (i, j) in enumerate(plan.folds):
        t = len(plan.pairs) + f
        packed[t * TILE : (t + 1) * TILE, :] = jnp.where(above_mask(TILE), tile(i, i), tile(j, j))
        line = jnp.sum(jnp.where(eye_mask(TILE), tile(i, i), 0.0), axis=0, keepdims=True)
        packed[plan.diagonals + f : plan.diagonals + f + 1, :] = line
    me = plan.me()

    def copy(part, own):
        ref = keep_ref if own else send_ref
        ref[plan.rows(part, me), :] = packed[part * plan.chunk : (part + 1) * plan.chunk, :]

    plan.halves(me, copy)


def gram(plan, sketch):
    rows, width = sketch.shape
    half = width // 2
    return pl.pallas_call(
        functools.partial(gram_kernel, plan),
        in_specs=[pl.BlockSpec(memory_space=pl.ANY)],
        out_specs=[pl.BlockSpec(memory_space=pltpu.VMEM)] * 2,
        out_shape=[jax.ShapeDtypeStruct((plan.half, TILE), F32)] * 2,
        scratch_shapes=[
            pltpu.VMEM((rows, width), F32),
            pltpu.VMEM((4, half, width), BF16),
            pltpu.VMEM((4, width, half), BF16),
            pltpu.VMEM((width, width), F32),
            pltpu.VMEM((2 * plan.half, TILE), F32),
            pltpu.SemaphoreType.DMA((rows // half,)),
        ],
        compiler_params=pltpu.CompilerParams(vmem_limit_bytes=VMEM_LIMIT),
    )(sketch)


def share(plan, keep, send):
    own = keep + plan.swap(send, 1)
    for x, y in plan.stages:
        m = own.shape[0] // 4
        got = [plan.swap(own[d * m : (d + 1) * m], k) for d, k in ((1, y), (2, x), (3, x + y))]
        own = own[:m] + got[0] + got[1] + got[2]
    one, two = plan.z
    got = [plan.swap(own, z) for z in (one, two, one + two)]
    own = (own + got[0]) + (got[1] + got[2])
    pieces = [own]
    for x, y in reversed(plan.stages):
        got = [plan.swap(piece, mask) for mask in (y, x, x + y) for piece in pieces]
        pieces = pieces + got
    far = [plan.swap(piece, 1) for piece in pieces]
    return jnp.concatenate(pieces, axis=0), jnp.concatenate(far, axis=0)


def log_near(x):
    return jnp.where(x > 0.5, jnp.log1p(x - 1.0), jnp.log(x))


def fold(x):
    n = x.shape[0]
    return jnp.sum(x.reshape(n // 8, 8, x.shape[1]), axis=0)


def near_inverse(accs, a, o_ref, y_ref, r1_ref, r2_ref, acc_ref):
    n = a.shape[0]
    eye = eye_mask(n)
    diagonal = jnp.where(eye, a, 0.0)
    s_row = lax.rsqrt(jnp.sum(diagonal, axis=0, keepdims=True))
    s_col = lax.rsqrt(jnp.sum(diagonal, axis=1, keepdims=True))
    c = a * s_col * s_row
    norm = jnp.max(jnp.sum(jnp.abs(c), axis=0, keepdims=True), axis=1, keepdims=True)
    inv_norm = 1.0 / norm
    rho0 = 1.0 - inv_norm
    start = jnp.where(eye, 1.0 - rho0, 0.0) - c * inv_norm
    o_ref[...] = start
    for ref in (y_ref, r1_ref, r2_ref):
        ref[...] = jnp.zeros((n, n), F32)
    acc_ref[...] = fold(jnp.where(eye, LOG1P[1] * (start + rho0), 0.0))
    square0, square1, factor0, factor1 = accs

    def more(carry):
        return jnp.logical_and(carry[0] < MAX_SQUARINGS, carry[1] >= 1e-3)

    def body(carry):
        k, _, rho, xi = carry
        o = o_ref[...]
        y = y_ref[...]
        oh, ol = split(o)
        yh, yl = split(y)
        sums_of(
            [(oh, [(square0, oh), (square0, ol), (factor0, yh)])],
            [(ol, [(square1, oh), (factor1, yh)]), (oh, [(factor1, yl)])],
        )
        r1 = r1_ref[...]
        r = o + jnp.where(eye, rho, 0.0)
        w0 = LOG1P[1] + LOG1P[2] + jnp.where(k >= 1, LOG1P[4], 0.0) + jnp.where(k >= 2, LOG1P[8], 0.0)
        w1 = jnp.where(k >= 1, LOG1P[3], 0.0) + jnp.where(k >= 2, LOG1P[6], 0.0)
        acc_ref[...] += fold(r * (w0 * r + w1 * r1 + LOG1P[5] * r2_ref[...]))
        size = jnp.sum(fold(r * r))
        r2_ref[...] = r1
        r1_ref[...] = r
        o_ref[...] = (2.0 * rho) * o + pop_both(square0, square1)
        y_ref[...] = (1.0 + rho) * y + xi * o + pop_both(factor0, factor1)
        return k + 1, size, rho * rho, xi * (1.0 + rho)

    begin = (jnp.int32(0), jnp.float32(1e30), jnp.max(rho0), jnp.max(inv_norm))
    _, size, _, xi = lax.while_loop(more, body, begin)
    x = y_ref[...] + jnp.where(eye, xi, 0.0)
    rest = jnp.where(eye, 1.0, 0.0) - dot6(accs, c, x)
    sums_of([(rest.astype(BF16), [(square0, x.astype(BF16))])])
    x = x + pltpu.matmul_pop(square0)
    log_det = -n * log_near(inv_norm) - jnp.sum(acc_ref[...], keepdims=True) - 2.0 * jnp.sum(
        log_near(s_row), axis=1, keepdims=True
    )
    return x * s_col * s_row, log_det, size


def sweep(a_ref, c_ref, log_ref):
    n = a_ref.shape[0]
    eye = eye_mask(n)
    diagonal = jnp.where(eye, a_ref[...], 0.0)
    s_row = lax.rsqrt(jnp.sum(diagonal, axis=0, keepdims=True))
    s_col = lax.rsqrt(jnp.sum(diagonal, axis=1, keepdims=True))
    c_ref[...] = a_ref[...] * s_col * s_row
    log_ref[...] = -2.0 * jnp.sum(log_near(s_row), axis=1, keepdims=True)
    lane = lax.broadcasted_iota(jnp.int32, (1, n), 1)

    @pl.loop(0, n)
    def _(k):
        row = c_ref[pl.ds(k, 1), :]
        here = lane == k
        pivot = jnp.sum(jnp.where(here, row, 0.0), axis=1, keepdims=True)
        log_ref[...] += log_near(pivot)
        u = jnp.where(here, pivot - 1.0, row)
        column = jnp.broadcast_to(u, (8, n)).T[:, :1]
        outer = column * (u / pivot)
        c_ref[...] = c_ref[...] - outer
        c_ref[pl.ds(k, 1), :] = c_ref[pl.ds(k, 1), :] - jnp.where(here, 2.0, 0.0)

    c_ref[...] = -(c_ref[...] * s_col * s_row)


def solve_kernel(
    plan, rows_all, near_ref, far_ref, sketch_ref, out_ref, log_ref,
    packed, a_ref, x_ref, o_ref, y_ref, r1_ref, r2_ref, acc_ref,
    rows_ref, result, mats, parts, load_sem, store_sem,
):
    blocks = load_sem.shape[0]
    size = rows_ref.shape[0] // blocks

    def load(i):
        at = pl.ds(i * size, size)
        return pltpu.make_async_copy(sketch_ref.at[at], rows_ref.at[at], load_sem.at[i])

    def store(i):
        at = pl.ds(i * size, size)
        return pltpu.make_async_copy(result.at[at], out_ref.at[at], store_sem.at[i])

    for i in range(blocks):
        load(i).start()

    n = a_ref.shape[0]
    m = n // 2
    me = plan.me()

    def copy(part, own):
        ref = near_ref if own else far_ref
        packed[part * plan.chunk : (part + 1) * plan.chunk, :] = ref[plan.rows(part, me), :]

    plan.halves(me, copy)

    scale = jnp.float32(1.0 / rows_all)
    unit = jnp.where(eye_mask(TILE), 1.0, 0.0)
    rows = lambda i: slice(i * TILE, (i + 1) * TILE)
    for t, (i, j) in enumerate(plan.pairs):
        tile = packed[rows(t), :] * scale
        a_ref[rows(i), rows(j)] = tile
        a_ref[rows(j), rows(i)] = tile.T
    above = above_mask(TILE)
    for f, (i, j) in enumerate(plan.folds):
        tile = packed[rows(len(plan.pairs) + f), :] * scale
        line = packed[plan.diagonals + f : plan.diagonals + f + 1, :] * scale
        mixed = jnp.where(eye_mask(TILE), line, jnp.where(above, tile, tile.T))
        a_ref[rows(i), rows(i)] = mixed + unit
        a_ref[rows(j), rows(j)] = jnp.where(above, tile.T, tile) + unit

    bufs = (o_ref, y_ref, r1_ref, r2_ref, acc_ref)

    def invert(*accs):
        x11, log1, size1 = near_inverse(accs, a_ref[:m, :m], *bufs)
        t12 = dot6(accs, x11, a_ref[:m, m:])
        schur = a_ref[m:, m:] - dot6(accs, a_ref[m:, :m], t12)
        x_ref[:m, :m] = x11
        x_ref[:m, m:] = t12
        x22, log2, size2 = near_inverse(accs, schur, *bufs)
        t12 = x_ref[:m, m:]
        x12 = -dot6(accs, t12, x22)
        x_ref[:m, :m] = x_ref[:m, :m] - dot6(accs, x12, t12.T)
        x_ref[:m, m:] = x12
        x_ref[m:, :m] = x12.T
        x_ref[m:, m:] = x22
        log_ref[...] = log1 + log2
        good = jnp.logical_and(size1 < 1e-3, size2 < 1e-3)

        @pl.when(jnp.logical_not(good))
        def _():
            sweep(a_ref, x_ref, log_ref)

    pl.run_scoped(invert, *[pltpu.ACC(unit)((m, m), F32) for unit in (0, 1, 0, 1)])
    log_ref[...] = log_ref[...] / n
    eye = eye_mask(n)
    diagonal = jnp.sum(jnp.where(eye, x_ref[...], 0.0), axis=0, keepdims=True)
    high, low = split(jnp.where(eye, 0.0, x_ref[...]))
    mats[0] = high
    mats[1] = low
    for i in range(blocks):
        load(i).wait()

    def prepare(i):
        h, l = split(rows_ref[i * size : (i + 1) * size, :])
        parts[2 * (i % 2)] = h
        parts[2 * (i % 2) + 1] = l

    steps = [(i, k, which) for i in range(blocks) for k in range(2) for which in range(2)]

    def push(step):
        _, k, which = steps[step]
        for unit in range(2):
            tile = mats[which, k * m : (k + 1) * m, unit * m : (unit + 1) * m]
            pltpu.matmul_push_rhs(tile, which, unit)

    def products(*accs):
        def finish(i):
            at = slice(i * size, (i + 1) * size)
            for unit, acc in enumerate(accs[2 * (i % 2) : 2 * (i % 2) + 2]):
                cols = slice(unit * m, (unit + 1) * m)
                result[at, cols] = rows_ref[at, cols] * diagonal[:, cols] + pltpu.matmul_pop(acc)
            store(i).start()

        push(0)
        push(1)
        prepare(0)
        for step, (i, k, which) in enumerate(steps):
            h, l = 2 * (i % 2), 2 * (i % 2) + 1
            mine = accs[h : h + 2]
            cols = slice(k * m, (k + 1) * m)
            for acc in mine:
                multiply(acc, parts[h, :, cols], which)
            if which == 0:
                for acc in mine:
                    multiply(acc, parts[l, :, cols])
            if step + 2 < len(steps):
                push(step + 2)
            if k == 0 and which == 0 and i > 0:
                finish(i - 1)
            if k == 0 and which == 1 and i + 1 < blocks:
                prepare(i + 1)
        finish(blocks - 1)

    pl.run_scoped(products, *[pltpu.ACC(unit)((size, m), F32) for unit in (0, 1, 0, 1)])
    for i in range(blocks):
        store(i).wait()


def solve(plan, sketch, near, far):
    rows, width = sketch.shape
    m = width // 2
    block = min(512, rows)
    vmem = pl.BlockSpec(memory_space=pltpu.VMEM)
    hbm = pl.BlockSpec(memory_space=pl.ANY)
    return pl.pallas_call(
        functools.partial(solve_kernel, plan, rows * plan.n),
        in_specs=[vmem, vmem, hbm],
        out_specs=[hbm, vmem],
        out_shape=[
            jax.ShapeDtypeStruct((rows, width), F32),
            jax.ShapeDtypeStruct((1, 1), F32),
        ],
        scratch_shapes=[
            pltpu.VMEM((2 * plan.half, TILE), F32),
            pltpu.VMEM((width, width), F32),
            pltpu.VMEM((width, width), F32),
            pltpu.VMEM((m, m), F32),
            pltpu.VMEM((m, m), F32),
            pltpu.VMEM((m, m), F32),
            pltpu.VMEM((m, m), F32),
            pltpu.VMEM((8, m), F32),
            pltpu.VMEM((rows, width), F32),
            pltpu.VMEM((rows, width), F32),
            pltpu.VMEM((2, width, width), BF16),
            pltpu.VMEM((4, block, width), BF16),
            pltpu.SemaphoreType.DMA((rows // block,)),
            pltpu.SemaphoreType.DMA((rows // block,)),
        ],
        compiler_params=pltpu.CompilerParams(vmem_limit_bytes=VMEM_LIMIT),
    )(near, far, sketch)


def solution(mesh):
    nrow, ncol = mesh.shape["crow"], mesh.shape["ccol"]

    def on_device(sketch):
        plan = Plan(nrow, ncol, sketch.shape[1])
        keep, send = gram(plan, sketch)
        near, far = share(plan, keep, send)
        basis, log_mean = solve(plan, sketch, near, far)
        return basis, log_mean[0, 0]

    return jax.shard_map(
        on_device,
        mesh=mesh,
        in_specs=(P(AXES, None),),
        out_specs=(P(AXES, None), P()),
        check_vma=False,
    )
```

```python
import functools

import jax
import jax.numpy as jnp
from jax import lax
from jax.experimental import pallas as pl
from jax.experimental.pallas import tpu as pltpu
from jax.sharding import PartitionSpec as P

AXES = ("crow", "ccol")
TILE = 128
F32 = jnp.float32
BF16 = jnp.bfloat16
LOG1P = {
    1: 0.9999739192217169,
    2: -0.49928683013429037,
    3: 0.32664225835205063,
    4: -0.21934280863425915,
    5: 0.12031934947180563,
    6: -0.037875575885947615,
    8: 0.0027171687390490683,
}
MAX_SQUARINGS = 12
VMEM_LIMIT = 48 * 1024 * 1024


def split(x):
    high = x.astype(BF16)
    return high, (x - high.astype(F32)).astype(BF16)


def split3(x):
    high = x.astype(BF16)
    rest = x - high.astype(F32)
    middle = rest.astype(BF16)
    return high, middle, (rest - middle.astype(F32)).astype(BF16)


def multiply(acc, left, staged=None):
    pltpu.matmul_acc_lhs(acc, left, load_staged_rhs=staged)


def sums_of(*units):
    for unit, terms in enumerate(units):
        for t, (tile, _) in enumerate(terms[:2]):
            pltpu.matmul_push_rhs(tile, t, unit)
    for t in range(max(len(terms) for terms in units)):
        for unit, terms in enumerate(units):
            if t < len(terms):
                for n, (acc, left) in enumerate(terms[t][1]):
                    multiply(acc, left, t % 2 if n == 0 else None)
                if t + 2 < len(terms):
                    pltpu.matmul_push_rhs(terms[t + 2][0], t % 2, unit)


def pop_both(one, two):
    return pltpu.matmul_pop(one) + pltpu.matmul_pop(two)


def dot6(accs, a, b):
    one, two = accs[:2]
    a0, a1, a2 = split3(a)
    b0, b1, b2 = split3(b)
    sums_of(
        [(b0, [(one, a0), (one, a1), (one, a2)])],
        [(b1, [(two, a0), (two, a1)]), (b2, [(two, a0)])],
    )
    return pop_both(one, two)


def eye_mask(n):
    return lax.broadcasted_iota(jnp.int32, (n, n), 0) == lax.broadcasted_iota(jnp.int32, (n, n), 1)


def above_mask(n):
    return lax.broadcasted_iota(jnp.int32, (n, n), 0) < lax.broadcasted_iota(jnp.int32, (n, n), 1)


class Plan:
    def __init__(self, nrow, ncol, width):
        self.ncol = ncol
        self.n = nrow * ncol
        self.parts = self.n // 4
        bits = [1 << b for b in range(1, self.n.bit_length() - 1)]
        y = [b for b in bits if b < ncol]
        x = [b for b in bits if ncol <= b < self.parts]
        self.z = [b for b in bits if b >= self.parts]
        self.stages = list(zip(x, y))
        tiles = width // TILE
        self.pairs = [(i, j) for i in range(tiles) for j in range(i + 1, tiles)]
        self.folds = [(i, i + 1) for i in range(0, tiles, 2)]
        self.diagonals = (len(self.pairs) + len(self.folds)) * TILE
        self.chunk = 8 * pl.cdiv(self.diagonals + 8, 8 * self.parts)
        self.half = self.chunk * self.parts // 2

    def me(self):
        return lax.axis_index("crow") * self.ncol + lax.axis_index("ccol")

    def rows(self, part, me):
        order = 0
        for mask in sum(self.stages, ()):
            here = jnp.bitwise_and(jnp.bitwise_xor(part, me), mask) // mask
            order = 2 * order + here
        return pl.ds(pl.multiple_of(order * self.chunk, 8), self.chunk)

    def halves(self, me, copy):
        for core in range(2):

            @pl.when(jnp.bitwise_and(me, 1) == core)
            def _():
                for part in range(self.parts):
                    copy(part, part & 1 == core)

    def swap(self, x, mask):
        return lax.ppermute(x, AXES, [(i, i ^ mask) for i in range(self.n)])


def gram_kernel(
    plan, sketch_ref, keep_ref, send_ref,
    rows_ref, flat, turned, whole, packed, load_sem,
):
    blocks = load_sem.shape[0]
    size = rows_ref.shape[0] // blocks
    width = rows_ref.shape[1]
    half = width // 2
    first, second = slice(0, half), slice(half, width)

    def load(i):
        at = pl.ds(i * size, size)
        return pltpu.make_async_copy(sketch_ref.at[at], rows_ref.at[at], load_sem.at[i])

    def prepare(i):
        if i != 1 and i & (i - 1) == 0:
            for j in range(i, min(max(2 * i, 2), blocks)):
                load(j).wait()
        h, l = split(rows_ref[i * size : (i + 1) * size, :])
        flat[2 * (i % 2)] = h
        flat[2 * (i % 2) + 1] = l
        turned[2 * (i % 2)] = h.T
        turned[2 * (i % 2) + 1] = l.T

    def push(slot, staged):
        pltpu.matmul_push_rhs(flat[slot, :, first], staged, 0)
        pltpu.matmul_push_rhs(flat[slot, :, second], staged, 1)

    for i in range(blocks):
        load(i).start()
    prepare(0)

    def sums(s00, z10, c00, z01, s11, c11):
        push(0, 0)
        for i in range(blocks):
            h, l = 2 * (i % 2), 2 * (i % 2) + 1
            push(l, 1)
            multiply(s00, turned[h, first, :], 0)
            multiply(s11, turned[h, second, :], 0)
            multiply(z10, turned[h, second, :])
            if i + 1 < blocks:
                prepare(i + 1)
                push(2 * ((i + 1) % 2), 0)
            multiply(s00, turned[l, first, :], 1)
            multiply(z01, turned[l, first, :], 1)
            multiply(c00, turned[h, first, :])
            multiply(z01, turned[h, first, :])
            multiply(z10, turned[h, second, :])
            multiply(s11, turned[l, second, :])
            multiply(c11, turned[h, second, :])

        cross = pltpu.matmul_pop(c00)
        whole[first, first] = pltpu.matmul_pop(s00) + cross + cross.T
        whole[first, second] = pltpu.matmul_pop(z01) + pltpu.matmul_pop(z10).T
        cross = pltpu.matmul_pop(c11)
        whole[second, second] = pltpu.matmul_pop(s11) + cross + cross.T

    square = (half, half)
    units = (0, 0, 0, 1, 1, 1)
    pl.run_scoped(sums, *[pltpu.ACC(unit)(square, F32) for unit in units])
    tile = lambda i, j: whole[i * TILE : (i + 1) * TILE, j * TILE : (j + 1) * TILE]
    packed[plan.diagonals :, :] = jnp.zeros_like(packed[plan.diagonals :, :])
    for t, (i, j) in enumerate(plan.pairs):
        packed[t * TILE : (t + 1) * TILE, :] = tile(i, j)
    for f, (i, j) in enumerate(plan.folds):
        t = len(plan.pairs) + f
        packed[t * TILE : (t + 1) * TILE, :] = jnp.where(above_mask(TILE), tile(i, i), tile(j, j))
        line = jnp.sum(jnp.where(eye_mask(TILE), tile(i, i), 0.0), axis=0, keepdims=True)
        packed[plan.diagonals + f : plan.diagonals + f + 1, :] = line
    me = plan.me()

    def copy(part, own):
        ref = keep_ref if own else send_ref
        ref[plan.rows(part, me), :] = packed[part * plan.chunk : (part + 1) * plan.chunk, :]

    plan.halves(me, copy)


def gram(plan, sketch):
    rows, width = sketch.shape
    half = width // 2
    return pl.pallas_call(
        functools.partial(gram_kernel, plan),
        in_specs=[pl.BlockSpec(memory_space=pl.ANY)],
        out_specs=[pl.BlockSpec(memory_space=pltpu.VMEM)] * 2,
        out_shape=[jax.ShapeDtypeStruct((plan.half, TILE), F32)] * 2,
        scratch_shapes=[
            pltpu.VMEM((rows, width), F32),
            pltpu.VMEM((4, half, width), BF16),
            pltpu.VMEM((4, width, half), BF16),
            pltpu.VMEM((width, width), F32),
            pltpu.VMEM((2 * plan.half, TILE), F32),
            pltpu.SemaphoreType.DMA((rows // half,)),
        ],
        compiler_params=pltpu.CompilerParams(vmem_limit_bytes=VMEM_LIMIT),
    )(sketch)


def share(plan, keep, send):
    own = None
    for x, y in plan.stages:
        m = (keep if own is None else own).shape[0] // 4
        rows = [slice(d * m, (d + 1) * m) for d in range(4)]
        if own is None:
            cut = [keep[r] + plan.swap(send[r], 1) for r in rows]
        else:
            cut = [own[r] for r in rows]
        got = [plan.swap(piece, mask) for piece, mask in zip(cut[1:], (y, x, x + y))]
        own = cut[0] + got[0] + got[1] + got[2]
    one, two = plan.z
    got = [plan.swap(own, z) for z in (one, two, one + two)]
    own = (own + got[0]) + (got[1] + got[2])
    pieces = [own]
    for x, y in reversed(plan.stages):
        got = [plan.swap(piece, mask) for mask in (y, x, x + y) for piece in pieces]
        pieces = pieces + got
    far = [plan.swap(piece, 1) for piece in pieces]
    return jnp.concatenate(pieces, axis=0), jnp.concatenate(far, axis=0)


def fold(x):
    n = x.shape[0]
    return jnp.sum(x.reshape(n // 8, 8, x.shape[1]), axis=0)


def near_inverse(accs, a, o_ref, y_ref, r1_ref, r2_ref, acc_ref):
    n = a.shape[0]
    eye = eye_mask(n)
    diagonal = jnp.where(eye, a, 0.0)
    s_row = lax.rsqrt(jnp.sum(diagonal, axis=0, keepdims=True))
    s_col = lax.rsqrt(jnp.sum(diagonal, axis=1, keepdims=True))
    c = a * s_col * s_row
    norm = jnp.max(jnp.sum(jnp.abs(c), axis=0, keepdims=True), axis=1, keepdims=True)
    inv_norm = 1.0 / norm
    rho0 = 1.0 - inv_norm
    start = jnp.where(eye, 1.0 - rho0, 0.0) - c * inv_norm
    o_ref[...] = start
    for ref in (y_ref, r1_ref, r2_ref):
        ref[...] = jnp.zeros((n, n), F32)
    acc_ref[...] = fold(jnp.where(eye, LOG1P[1] * (start + rho0), 0.0))
    square0, square1, factor0, factor1 = accs

    def more(carry):
        return jnp.logical_and(carry[0] < MAX_SQUARINGS, carry[1] >= 1e-3)

    def body(carry):
        k, _, rho, xi = carry
        o = o_ref[...]
        y = y_ref[...]
        oh, ol = split(o)
        yh, yl = split(y)
        sums_of(
            [(oh, [(square0, oh), (square0, ol), (factor0, yh)])],
            [(ol, [(square1, oh), (factor1, yh)]), (oh, [(factor1, yl)])],
        )
        r1 = r1_ref[...]
        r = o + jnp.where(eye, rho, 0.0)
        w0 = LOG1P[1] + LOG1P[2] + jnp.where(k >= 1, LOG1P[4], 0.0) + jnp.where(k >= 2, LOG1P[8], 0.0)
        w1 = jnp.where(k >= 1, LOG1P[3], 0.0) + jnp.where(k >= 2, LOG1P[6], 0.0)
        acc_ref[...] += fold(r * (w0 * r + w1 * r1 + LOG1P[5] * r2_ref[...]))
        size = jnp.sum(fold(r * r))
        r2_ref[...] = r1
        r1_ref[...] = r
        o_ref[...] = (2.0 * rho) * o + pop_both(square0, square1)
        y_ref[...] = (1.0 + rho) * y + xi * o + pop_both(factor0, factor1)
        return k + 1, size, rho * rho, xi * (1.0 + rho)

    begin = (jnp.int32(0), jnp.float32(1e30), jnp.max(rho0), jnp.max(inv_norm))
    _, size, _, xi = lax.while_loop(more, body, begin)
    x = y_ref[...] + jnp.where(eye, xi, 0.0)
    rest = jnp.where(eye, 1.0, 0.0) - dot6(accs, c, x)
    sums_of([(rest.astype(BF16), [(square0, x.astype(BF16))])])
    x = x + pltpu.matmul_pop(square0)
    log_det = n * jnp.log(norm) - jnp.sum(acc_ref[...], keepdims=True) - 2.0 * jnp.sum(
        jnp.log(s_row), axis=1, keepdims=True
    )
    return x * s_col * s_row, log_det, size


def sweep(a_ref, c_ref, log_ref):
    n = a_ref.shape[0]
    eye = eye_mask(n)
    diagonal = jnp.where(eye, a_ref[...], 0.0)
    s_row = lax.rsqrt(jnp.sum(diagonal, axis=0, keepdims=True))
    s_col = lax.rsqrt(jnp.sum(diagonal, axis=1, keepdims=True))
    c_ref[...] = a_ref[...] * s_col * s_row
    log_ref[...] = -2.0 * jnp.sum(jnp.log(s_row), axis=1, keepdims=True)
    lane = lax.broadcasted_iota(jnp.int32, (1, n), 1)

    @pl.loop(0, n)
    def _(k):
        row = c_ref[pl.ds(k, 1), :]
        here = lane == k
        pivot = jnp.sum(jnp.where(here, row, 0.0), axis=1, keepdims=True)
        log_ref[...] += jnp.log(pivot)
        u = jnp.where(here, pivot - 1.0, row)
        column = jnp.broadcast_to(u, (8, n)).T[:, :1]
        outer = column * (u / pivot)
        c_ref[...] = c_ref[...] - outer
        c_ref[pl.ds(k, 1), :] = c_ref[pl.ds(k, 1), :] - jnp.where(here, 2.0, 0.0)

    c_ref[...] = -(c_ref[...] * s_col * s_row)


def solve_kernel(
    plan, rows_all, near_ref, far_ref, sketch_ref, out_ref, log_ref,
    packed, a_ref, x_ref, o_ref, y_ref, r1_ref, r2_ref, acc_ref,
    rows_ref, result, mats, parts, load_sem, store_sem,
):
    blocks = load_sem.shape[0]
    size = rows_ref.shape[0] // blocks

    def load(i):
        at = pl.ds(i * size, size)
        return pltpu.make_async_copy(sketch_ref.at[at], rows_ref.at[at], load_sem.at[i])

    def store(i):
        at = pl.ds(i * size, size)
        return pltpu.make_async_copy(result.at[at], out_ref.at[at], store_sem.at[i])

    for i in range(blocks):
        load(i).start()

    n = a_ref.shape[0]
    m = n // 2
    me = plan.me()

    def copy(part, own):
        ref = near_ref if own else far_ref
        packed[part * plan.chunk : (part + 1) * plan.chunk, :] = ref[plan.rows(part, me), :]

    plan.halves(me, copy)

    scale = jnp.float32(1.0 / rows_all)
    unit = jnp.where(eye_mask(TILE), 1.0, 0.0)
    rows = lambda i: slice(i * TILE, (i + 1) * TILE)
    for t, (i, j) in enumerate(plan.pairs):
        tile = packed[rows(t), :] * scale
        a_ref[rows(i), rows(j)] = tile
        a_ref[rows(j), rows(i)] = tile.T
    above = above_mask(TILE)
    for f, (i, j) in enumerate(plan.folds):
        tile = packed[rows(len(plan.pairs) + f), :] * scale
        line = packed[plan.diagonals + f : plan.diagonals + f + 1, :] * scale
        mixed = jnp.where(eye_mask(TILE), line, jnp.where(above, tile, tile.T))
        a_ref[rows(i), rows(i)] = mixed + unit
        a_ref[rows(j), rows(j)] = jnp.where(above, tile.T, tile) + unit

    bufs = (o_ref, y_ref, r1_ref, r2_ref, acc_ref)

    def invert(*accs):
        x11, log1, size1 = near_inverse(accs, a_ref[:m, :m], *bufs)
        t12 = dot6(accs, x11, a_ref[:m, m:])
        schur = a_ref[m:, m:] - dot6(accs, a_ref[m:, :m], t12)
        x_ref[:m, :m] = x11
        x_ref[:m, m:] = t12
        x22, log2, size2 = near_inverse(accs, schur, *bufs)
        t12 = x_ref[:m, m:]
        x12 = -dot6(accs, t12, x22)
        x_ref[:m, :m] = x_ref[:m, :m] - dot6(accs, x12, t12.T)
        x_ref[:m, m:] = x12
        x_ref[m:, :m] = x12.T
        x_ref[m:, m:] = x22
        log_ref[...] = log1 + log2
        good = jnp.logical_and(size1 < 1e-3, size2 < 1e-3)

        @pl.when(jnp.logical_not(good))
        def _():
            sweep(a_ref, x_ref, log_ref)

    pl.run_scoped(invert, *[pltpu.ACC(unit)((m, m), F32) for unit in (0, 1, 0, 1)])
    log_ref[...] = log_ref[...] / n
    eye = eye_mask(n)
    diagonal = jnp.sum(jnp.where(eye, x_ref[...], 0.0), axis=0, keepdims=True)
    high, low = split(jnp.where(eye, 0.0, x_ref[...]))
    mats[0] = high
    mats[1] = low
    for i in range(blocks):
        load(i).wait()

    def prepare(i):
        h, l = split(rows_ref[i * size : (i + 1) * size, :])
        parts[2 * (i % 2)] = h
        parts[2 * (i % 2) + 1] = l

    steps = [(i, k, which) for i in range(blocks) for k in range(2) for which in range(2)]

    def push(step):
        _, k, which = steps[step]
        for unit in range(2):
            tile = mats[which, k * m : (k + 1) * m, unit * m : (unit + 1) * m]
            pltpu.matmul_push_rhs(tile, which, unit)

    def products(*accs):
        def finish(i):
            at = slice(i * size, (i + 1) * size)
            for unit, acc in enumerate(accs[2 * (i % 2) : 2 * (i % 2) + 2]):
                cols = slice(unit * m, (unit + 1) * m)
                result[at, cols] = rows_ref[at, cols] * diagonal[:, cols] + pltpu.matmul_pop(acc)
            store(i).start()

        push(0)
        push(1)
        prepare(0)
        for step, (i, k, which) in enumerate(steps):
            h, l = 2 * (i % 2), 2 * (i % 2) + 1
            mine = accs[h : h + 2]
            cols = slice(k * m, (k + 1) * m)
            for acc in mine:
                multiply(acc, parts[h, :, cols], which)
            if which == 0:
                for acc in mine:
                    multiply(acc, parts[l, :, cols])
            if step + 2 < len(steps):
                push(step + 2)
            if k == 0 and which == 0 and i > 0:
                finish(i - 1)
            if k == 0 and which == 1 and i + 1 < blocks:
                prepare(i + 1)
        finish(blocks - 1)

    pl.run_scoped(products, *[pltpu.ACC(unit)((size, m), F32) for unit in (0, 1, 0, 1)])
    for i in range(blocks):
        store(i).wait()


def solve(plan, sketch, near, far):
    rows, width = sketch.shape
    m = width // 2
    block = min(512, rows)
    vmem = pl.BlockSpec(memory_space=pltpu.VMEM)
    hbm = pl.BlockSpec(memory_space=pl.ANY)
    return pl.pallas_call(
        functools.partial(solve_kernel, plan, rows * plan.n),
        in_specs=[vmem, vmem, hbm],
        out_specs=[hbm, vmem],
        out_shape=[
            jax.ShapeDtypeStruct((rows, width), F32),
            jax.ShapeDtypeStruct((1, 1), F32),
        ],
        scratch_shapes=[
            pltpu.VMEM((2 * plan.half, TILE), F32),
            pltpu.VMEM((width, width), F32),
            pltpu.VMEM((width, width), F32),
            pltpu.VMEM((m, m), F32),
            pltpu.VMEM((m, m), F32),
            pltpu.VMEM((m, m), F32),
            pltpu.VMEM((m, m), F32),
            pltpu.VMEM((8, m), F32),
            pltpu.VMEM((rows, width), F32),
            pltpu.VMEM((rows, width), F32),
            pltpu.VMEM((2, width, width), BF16),
            pltpu.VMEM((4, block, width), BF16),
            pltpu.SemaphoreType.DMA((rows // block,)),
            pltpu.SemaphoreType.DMA((rows // block,)),
        ],
        compiler_params=pltpu.CompilerParams(vmem_limit_bytes=VMEM_LIMIT),
    )(near, far, sketch)


def solution(mesh):
    nrow, ncol = mesh.shape["crow"], mesh.shape["ccol"]

    def on_device(sketch):
        plan = Plan(nrow, ncol, sketch.shape[1])
        keep, send = gram(plan, sketch)
        near, far = share(plan, keep, send)
        basis, log_mean = solve(plan, sketch, near, far)
        return basis, log_mean[0, 0]

    return jax.shard_map(
        on_device,
        mesh=mesh,
        in_specs=(P(AXES, None),),
        out_specs=(P(AXES, None), P()),
        check_vma=False,
    )
```

```python
import functools

import jax
import jax.numpy as jnp
from jax import lax
from jax.experimental import pallas as pl
from jax.experimental.pallas import tpu as pltpu
from jax.sharding import PartitionSpec as P

AXES = ("crow", "ccol")
TILE = 128
F32 = jnp.float32
BF16 = jnp.bfloat16
LOG1P = {
    1: 0.9999739192217169,
    2: -0.49928683013429037,
    3: 0.32664225835205063,
    4: -0.21934280863425915,
    5: 0.12031934947180563,
    6: -0.037875575885947615,
    8: 0.0027171687390490683,
}
MAX_SQUARINGS = 12
VMEM_LIMIT = 48 * 1024 * 1024


def split(x):
    high = x.astype(BF16)
    return high, (x - high.astype(F32)).astype(BF16)


def split3(x):
    high = x.astype(BF16)
    rest = x - high.astype(F32)
    middle = rest.astype(BF16)
    return high, middle, (rest - middle.astype(F32)).astype(BF16)


def multiply(acc, left, staged=None):
    pltpu.matmul_acc_lhs(acc, left, load_staged_rhs=staged)


def sums_of(*units):
    for unit, terms in enumerate(units):
        for t, (tile, _) in enumerate(terms[:2]):
            pltpu.matmul_push_rhs(tile, t, unit)
    for t in range(max(len(terms) for terms in units)):
        for unit, terms in enumerate(units):
            if t < len(terms):
                for n, (acc, left) in enumerate(terms[t][1]):
                    multiply(acc, left, t % 2 if n == 0 else None)
                if t + 2 < len(terms):
                    pltpu.matmul_push_rhs(terms[t + 2][0], t % 2, unit)


def pop_both(one, two):
    return pltpu.matmul_pop(one) + pltpu.matmul_pop(two)


def dot6(accs, a, b):
    one, two = accs[:2]
    a0, a1, a2 = split3(a)
    b0, b1, b2 = split3(b)
    sums_of(
        [(b0, [(one, a0), (one, a1), (one, a2)])],
        [(b1, [(two, a0), (two, a1)]), (b2, [(two, a0)])],
    )
    return pop_both(one, two)


def eye_mask(n):
    return lax.broadcasted_iota(jnp.int32, (n, n), 0) == lax.broadcasted_iota(jnp.int32, (n, n), 1)


def above_mask(n):
    return lax.broadcasted_iota(jnp.int32, (n, n), 0) < lax.broadcasted_iota(jnp.int32, (n, n), 1)


class Plan:
    def __init__(self, nrow, ncol, width):
        self.ncol = ncol
        self.n = nrow * ncol
        self.parts = self.n // 4
        bits = [1 << b for b in range(1, self.n.bit_length() - 1)]
        y = [b for b in bits if b < ncol]
        x = [b for b in bits if ncol <= b < self.parts]
        self.z = [b for b in bits if b >= self.parts]
        self.stages = list(zip(x, y))
        tiles = width // TILE
        self.pairs = [(i, j) for i in range(tiles) for j in range(i + 1, tiles)]
        self.folds = [(i, i + 1) for i in range(0, tiles, 2)]
        self.diagonals = (len(self.pairs) + len(self.folds)) * TILE
        self.chunk = 8 * pl.cdiv(self.diagonals + 8, 8 * self.parts)
        self.half = self.chunk * self.parts // 2

    def me(self):
        return lax.axis_index("crow") * self.ncol + lax.axis_index("ccol")

    def rows(self, part, me):
        order = 0
        for mask in sum(self.stages, ()):
            here = jnp.bitwise_and(jnp.bitwise_xor(part, me), mask) // mask
            order = 2 * order + here
        return pl.ds(pl.multiple_of(order * self.chunk, 8), self.chunk)

    def halves(self, me, copy):
        for core in range(2):

            @pl.when(jnp.bitwise_and(me, 1) == core)
            def _():
                for part in range(self.parts):
                    copy(part, part & 1 == core)

    def swap(self, x, mask):
        return lax.ppermute(x, AXES, [(i, i ^ mask) for i in range(self.n)])


def gram_kernel(
    plan, sketch_ref, keep_ref, send_ref,
    rows_ref, flat, turned, whole, packed, load_sem,
):
    blocks = load_sem.shape[0]
    size = rows_ref.shape[0] // blocks
    width = rows_ref.shape[1]
    half = width // 2
    first, second = slice(0, half), slice(half, width)

    def load(i):
        at = pl.ds(i * size, size)
        return pltpu.make_async_copy(sketch_ref.at[at], rows_ref.at[at], load_sem.at[i])

    def prepare(i):
        if i != 1 and i & (i - 1) == 0:
            for j in range(i, min(max(2 * i, 2), blocks)):
                load(j).wait()
        h, l = split(rows_ref[i * size : (i + 1) * size, :])
        flat[2 * (i % 2)] = h
        flat[2 * (i % 2) + 1] = l
        turned[2 * (i % 2)] = h.T
        turned[2 * (i % 2) + 1] = l.T

    def push(slot, staged):
        pltpu.matmul_push_rhs(flat[slot, :, first], staged, 0)
        pltpu.matmul_push_rhs(flat[slot, :, second], staged, 1)

    for i in range(blocks):
        load(i).start()
    prepare(0)

    def sums(s00, z10, c00, z01, s11, c11):
        push(0, 0)
        for i in range(blocks):
            h, l = 2 * (i % 2), 2 * (i % 2) + 1
            push(l, 1)
            multiply(s00, turned[h, first, :], 0)
            multiply(s11, turned[h, second, :], 0)
            multiply(z10, turned[h, second, :])
            if i + 1 < blocks:
                prepare(i + 1)
                push(2 * ((i + 1) % 2), 0)
            multiply(s00, turned[l, first, :], 1)
            multiply(z01, turned[l, first, :], 1)
            multiply(c00, turned[h, first, :])
            multiply(z01, turned[h, first, :])
            multiply(z10, turned[h, second, :])
            multiply(s11, turned[l, second, :])
            multiply(c11, turned[h, second, :])

        cross = pltpu.matmul_pop(c00)
        whole[first, first] = pltpu.matmul_pop(s00) + cross + cross.T
        whole[first, second] = pltpu.matmul_pop(z01) + pltpu.matmul_pop(z10).T
        cross = pltpu.matmul_pop(c11)
        whole[second, second] = pltpu.matmul_pop(s11) + cross + cross.T

    square = (half, half)
    units = (0, 0, 0, 1, 1, 1)
    pl.run_scoped(sums, *[pltpu.ACC(unit)(square, F32) for unit in units])
    tile = lambda i, j: whole[i * TILE : (i + 1) * TILE, j * TILE : (j + 1) * TILE]
    packed[plan.diagonals :, :] = jnp.zeros_like(packed[plan.diagonals :, :])
    for t, (i, j) in enumerate(plan.pairs):
        packed[t * TILE : (t + 1) * TILE, :] = tile(i, j)
    for f, (i, j) in enumerate(plan.folds):
        t = len(plan.pairs) + f
        packed[t * TILE : (t + 1) * TILE, :] = jnp.where(above_mask(TILE), tile(i, i), tile(j, j))
        line = jnp.sum(jnp.where(eye_mask(TILE), tile(i, i), 0.0), axis=0, keepdims=True)
        packed[plan.diagonals + f : plan.diagonals + f + 1, :] = line
    me = plan.me()

    def copy(part, own):
        ref = keep_ref if own else send_ref
        ref[plan.rows(part, me), :] = packed[part * plan.chunk : (part + 1) * plan.chunk, :]

    plan.halves(me, copy)


def gram(plan, sketch):
    rows, width = sketch.shape
    half = width // 2
    return pl.pallas_call(
        functools.partial(gram_kernel, plan),
        in_specs=[pl.BlockSpec(memory_space=pl.ANY)],
        out_specs=[pl.BlockSpec(memory_space=pltpu.VMEM)] * 2,
        out_shape=[jax.ShapeDtypeStruct((plan.half, TILE), F32)] * 2,
        scratch_shapes=[
            pltpu.VMEM((rows, width), F32),
            pltpu.VMEM((4, half, width), BF16),
            pltpu.VMEM((4, width, half), BF16),
            pltpu.VMEM((width, width), F32),
            pltpu.VMEM((2 * plan.half, TILE), F32),
            pltpu.SemaphoreType.DMA((rows // half,)),
        ],
        compiler_params=pltpu.CompilerParams(vmem_limit_bytes=VMEM_LIMIT),
    )(sketch)


def share(plan, keep, send):
    own = keep + plan.swap(send, 1)
    for x, y in plan.stages:
        m = own.shape[0] // 4
        got = [plan.swap(own[d * m : (d + 1) * m], k) for d, k in ((1, y), (2, x), (3, x + y))]
        own = own[:m] + got[0] + got[1] + got[2]
    one, two = plan.z
    got = [plan.swap(own, z) for z in (one, two, one + two)]
    own = (own + got[0]) + (got[1] + got[2])
    pieces = [own]
    for x, y in reversed(plan.stages):
        got = [plan.swap(piece, mask) for mask in (y, x, x + y) for piece in pieces]
        pieces = pieces + got
    far = [plan.swap(piece, 1) for piece in pieces]
    return jnp.concatenate(pieces, axis=0), jnp.concatenate(far, axis=0)


def fold(x):
    n = x.shape[0]
    return jnp.sum(x.reshape(n // 8, 8, x.shape[1]), axis=0)


def near_inverse(accs, a, o_ref, y_ref, r1_ref, r2_ref, acc_ref):
    n = a.shape[0]
    eye = eye_mask(n)
    diagonal = jnp.where(eye, a, 0.0)
    s_row = lax.rsqrt(jnp.sum(diagonal, axis=0, keepdims=True))
    s_col = lax.rsqrt(jnp.sum(diagonal, axis=1, keepdims=True))
    c = a * s_col * s_row
    norm = jnp.max(jnp.sum(jnp.abs(c), axis=0, keepdims=True), axis=1, keepdims=True)
    inv_norm = 1.0 / norm
    rho0 = 1.0 - inv_norm
    start = jnp.where(eye, 1.0 - rho0, 0.0) - c * inv_norm
    o_ref[...] = start
    for ref in (y_ref, r1_ref, r2_ref):
        ref[...] = jnp.zeros((n, n), F32)
    acc_ref[...] = fold(jnp.where(eye, LOG1P[1] * (start + rho0), 0.0))
    square0, square1, factor0, factor1 = accs

    def more(carry):
        return jnp.logical_and(carry[0] < MAX_SQUARINGS, carry[1] >= 1e-3)

    def body(carry):
        k, _, rho, xi = carry
        o = o_ref[...]
        y = y_ref[...]
        oh, ol = split(o)
        yh, yl = split(y)
        sums_of(
            [(oh, [(square0, oh), (square0, ol), (factor0, yh)])],
            [(ol, [(square1, oh), (factor1, yh)]), (oh, [(factor1, yl)])],
        )
        r1 = r1_ref[...]
        r = o + jnp.where(eye, rho, 0.0)
        w0 = LOG1P[1] + LOG1P[2] + jnp.where(k >= 1, LOG1P[4], 0.0) + jnp.where(k >= 2, LOG1P[8], 0.0)
        w1 = jnp.where(k >= 1, LOG1P[3], 0.0) + jnp.where(k >= 2, LOG1P[6], 0.0)
        acc_ref[...] += fold(r * (w0 * r + w1 * r1 + LOG1P[5] * r2_ref[...]))
        size = jnp.sum(fold(r * r))
        r2_ref[...] = r1
        r1_ref[...] = r
        o_ref[...] = (2.0 * rho) * o + pop_both(square0, square1)
        y_ref[...] = (1.0 + rho) * y + xi * o + pop_both(factor0, factor1)
        return k + 1, size, rho * rho, xi * (1.0 + rho)

    begin = (jnp.int32(0), jnp.float32(1e30), jnp.max(rho0), jnp.max(inv_norm))
    _, size, _, xi = lax.while_loop(more, body, begin)
    x = y_ref[...] + jnp.where(eye, xi, 0.0)
    rest = jnp.where(eye, 1.0, 0.0) - dot6(accs, c, x)
    sums_of([(rest.astype(BF16), [(square0, x.astype(BF16))])])
    x = x + pltpu.matmul_pop(square0)
    log_det = n * jnp.log(norm) - jnp.sum(acc_ref[...], keepdims=True) - 2.0 * jnp.sum(
        jnp.log(s_row), axis=1, keepdims=True
    )
    return x * s_col * s_row, log_det, size


def sweep(a_ref, c_ref, log_ref):
    n = a_ref.shape[0]
    eye = eye_mask(n)
    diagonal = jnp.where(eye, a_ref[...], 0.0)
    s_row = lax.rsqrt(jnp.sum(diagonal, axis=0, keepdims=True))
    s_col = lax.rsqrt(jnp.sum(diagonal, axis=1, keepdims=True))
    c_ref[...] = a_ref[...] * s_col * s_row
    log_ref[...] = -2.0 * jnp.sum(jnp.log(s_row), axis=1, keepdims=True)
    lane = lax.broadcasted_iota(jnp.int32, (1, n), 1)

    @pl.loop(0, n)
    def _(k):
        row = c_ref[pl.ds(k, 1), :]
        here = lane == k
        pivot = jnp.sum(jnp.where(here, row, 0.0), axis=1, keepdims=True)
        log_ref[...] += jnp.log(pivot)
        u = jnp.where(here, pivot - 1.0, row)
        column = jnp.broadcast_to(u, (8, n)).T[:, :1]
        outer = column * (u / pivot)
        c_ref[...] = c_ref[...] - outer
        c_ref[pl.ds(k, 1), :] = c_ref[pl.ds(k, 1), :] - jnp.where(here, 2.0, 0.0)

    c_ref[...] = -(c_ref[...] * s_col * s_row)


def solve_kernel(
    plan, rows_all, near_ref, far_ref, sketch_ref, out_ref, log_ref,
    packed, a_ref, x_ref, o_ref, y_ref, r1_ref, r2_ref, acc_ref,
    rows_ref, result, mats, parts, load_sem, store_sem,
):
    blocks = load_sem.shape[0]
    size = rows_ref.shape[0] // blocks

    def load(i):
        at = pl.ds(i * size, size)
        return pltpu.make_async_copy(sketch_ref.at[at], rows_ref.at[at], load_sem.at[i])

    def store(i):
        at = pl.ds(i * size, size)
        return pltpu.make_async_copy(result.at[at], out_ref.at[at], store_sem.at[i])

    for i in range(blocks):
        load(i).start()

    n = a_ref.shape[0]
    m = n // 2
    me = plan.me()

    def copy(part, own):
        ref = near_ref if own else far_ref
        packed[part * plan.chunk : (part + 1) * plan.chunk, :] = ref[plan.rows(part, me), :]

    plan.halves(me, copy)

    scale = jnp.float32(1.0 / rows_all)
    unit = jnp.where(eye_mask(TILE), 1.0, 0.0)
    rows = lambda i: slice(i * TILE, (i + 1) * TILE)
    for t, (i, j) in enumerate(plan.pairs):
        tile = packed[rows(t), :] * scale
        a_ref[rows(i), rows(j)] = tile
        a_ref[rows(j), rows(i)] = tile.T
    above = above_mask(TILE)
    for f, (i, j) in enumerate(plan.folds):
        tile = packed[rows(len(plan.pairs) + f), :] * scale
        line = packed[plan.diagonals + f : plan.diagonals + f + 1, :] * scale
        mixed = jnp.where(eye_mask(TILE), line, jnp.where(above, tile, tile.T))
        a_ref[rows(i), rows(i)] = mixed + unit
        a_ref[rows(j), rows(j)] = jnp.where(above, tile.T, tile) + unit

    bufs = (o_ref, y_ref, r1_ref, r2_ref, acc_ref)

    def invert(*accs):
        x11, log1, size1 = near_inverse(accs, a_ref[:m, :m], *bufs)
        t12 = dot6(accs, x11, a_ref[:m, m:])
        schur = a_ref[m:, m:] - dot6(accs, a_ref[m:, :m], t12)
        x_ref[:m, :m] = x11
        x_ref[:m, m:] = t12
        x22, log2, size2 = near_inverse(accs, schur, *bufs)
        t12 = x_ref[:m, m:]
        x12 = -dot6(accs, t12, x22)
        x_ref[:m, :m] = x_ref[:m, :m] - dot6(accs, x12, t12.T)
        x_ref[:m, m:] = x12
        x_ref[m:, :m] = x12.T
        x_ref[m:, m:] = x22
        log_ref[...] = log1 + log2
        good = jnp.logical_and(size1 < 1e-3, size2 < 1e-3)

        @pl.when(jnp.logical_not(good))
        def _():
            sweep(a_ref, x_ref, log_ref)

    pl.run_scoped(invert, *[pltpu.ACC(unit)((m, m), F32) for unit in (0, 1, 0, 1)])
    log_ref[...] = log_ref[...] / n
    eye = eye_mask(n)
    diagonal = jnp.sum(jnp.where(eye, x_ref[...], 0.0), axis=0, keepdims=True)
    high, low = split(jnp.where(eye, 0.0, x_ref[...]))
    mats[0] = high
    mats[1] = low
    for i in range(blocks):
        load(i).wait()

    def prepare(i):
        h, l = split(rows_ref[i * size : (i + 1) * size, :])
        parts[2 * (i % 2)] = h
        parts[2 * (i % 2) + 1] = l

    steps = [(i, k, which) for i in range(blocks) for k in range(2) for which in range(2)]

    def push(step):
        _, k, which = steps[step]
        for unit in range(2):
            tile = mats[which, k * m : (k + 1) * m, unit * m : (unit + 1) * m]
            pltpu.matmul_push_rhs(tile, which, unit)

    def products(*accs):
        def finish(i):
            at = slice(i * size, (i + 1) * size)
            for unit, acc in enumerate(accs[2 * (i % 2) : 2 * (i % 2) + 2]):
                cols = slice(unit * m, (unit + 1) * m)
                result[at, cols] = rows_ref[at, cols] * diagonal[:, cols] + pltpu.matmul_pop(acc)
            store(i).start()

        push(0)
        push(1)
        prepare(0)
        for step, (i, k, which) in enumerate(steps):
            h, l = 2 * (i % 2), 2 * (i % 2) + 1
            mine = accs[h : h + 2]
            cols = slice(k * m, (k + 1) * m)
            for acc in mine:
                multiply(acc, parts[h, :, cols], which)
            if which == 0:
                for acc in mine:
                    multiply(acc, parts[l, :, cols])
            if step + 2 < len(steps):
                push(step + 2)
            if k == 0 and which == 0 and i > 0:
                finish(i - 1)
            if k == 0 and which == 1 and i + 1 < blocks:
                prepare(i + 1)
        finish(blocks - 1)

    pl.run_scoped(products, *[pltpu.ACC(unit)((size, m), F32) for unit in (0, 1, 0, 1)])
    for i in range(blocks):
        store(i).wait()


def solve(plan, sketch, near, far):
    rows, width = sketch.shape
    m = width // 2
    block = min(512, rows)
    vmem = pl.BlockSpec(memory_space=pltpu.VMEM)
    hbm = pl.BlockSpec(memory_space=pl.ANY)
    return pl.pallas_call(
        functools.partial(solve_kernel, plan, rows * plan.n),
        in_specs=[vmem, vmem, hbm],
        out_specs=[hbm, vmem],
        out_shape=[
            jax.ShapeDtypeStruct((rows, width), F32),
            jax.ShapeDtypeStruct((1, 1), F32),
        ],
        scratch_shapes=[
            pltpu.VMEM((2 * plan.half, TILE), F32),
            pltpu.VMEM((width, width), F32),
            pltpu.VMEM((width, width), F32),
            pltpu.VMEM((m, m), F32),
            pltpu.VMEM((m, m), F32),
            pltpu.VMEM((m, m), F32),
            pltpu.VMEM((m, m), F32),
            pltpu.VMEM((8, m), F32),
            pltpu.VMEM((rows, width), F32),
            pltpu.VMEM((rows, width), F32),
            pltpu.VMEM((2, width, width), BF16),
            pltpu.VMEM((4, block, width), BF16),
            pltpu.SemaphoreType.DMA((rows // block,)),
            pltpu.SemaphoreType.DMA((rows // block,)),
        ],
        compiler_params=pltpu.CompilerParams(vmem_limit_bytes=VMEM_LIMIT),
    )(near, far, sketch)


def solution(mesh):
    nrow, ncol = mesh.shape["crow"], mesh.shape["ccol"]

    def on_device(sketch):
        plan = Plan(nrow, ncol, sketch.shape[1])
        keep, send = gram(plan, sketch)
        near, far = share(plan, keep, send)
        basis, log_mean = solve(plan, sketch, near, far)
        return basis, log_mean[0, 0]

    return jax.shard_map(
        on_device,
        mesh=mesh,
        in_specs=(P(AXES, None),),
        out_specs=(P(AXES, None), P()),
        check_vma=False,
    )
```

```python
import functools

import jax
import jax.numpy as jnp
from jax import lax
from jax.experimental import pallas as pl
from jax.experimental.pallas import tpu as pltpu
from jax.sharding import PartitionSpec as P

AXES = ("crow", "ccol")
TILE = 128
F32 = jnp.float32
BF16 = jnp.bfloat16
LOG1P = {
    1: 0.9999739192217169,
    2: -0.49928683013429037,
    3: 0.32664225835205063,
    4: -0.21934280863425915,
    5: 0.12031934947180563,
    6: -0.037875575885947615,
    8: 0.0027171687390490683,
}
MAX_SQUARINGS = 12
VMEM_LIMIT = 48 * 1024 * 1024


def split(x):
    high = x.astype(BF16)
    return high, (x - high.astype(F32)).astype(BF16)


def split3(x):
    high = x.astype(BF16)
    rest = x - high.astype(F32)
    middle = rest.astype(BF16)
    return high, middle, (rest - middle.astype(F32)).astype(BF16)


def multiply(acc, left, staged=None):
    pltpu.matmul_acc_lhs(acc, left, load_staged_rhs=staged)


def sums_of(*units):
    for unit, terms in enumerate(units):
        for t, (tile, _) in enumerate(terms[:2]):
            pltpu.matmul_push_rhs(tile, t, unit)
    for t in range(max(len(terms) for terms in units)):
        for unit, terms in enumerate(units):
            if t < len(terms):
                for n, (acc, left) in enumerate(terms[t][1]):
                    multiply(acc, left, t % 2 if n == 0 else None)
                if t + 2 < len(terms):
                    pltpu.matmul_push_rhs(terms[t + 2][0], t % 2, unit)


def pop_both(one, two):
    return pltpu.matmul_pop(one) + pltpu.matmul_pop(two)


def dot6(accs, a, b):
    one, two = accs[:2]
    a0, a1, a2 = split3(a)
    b0, b1, b2 = split3(b)
    sums_of(
        [(b0, [(one, a0), (one, a1), (one, a2)])],
        [(b1, [(two, a0), (two, a1)]), (b2, [(two, a0)])],
    )
    return pop_both(one, two)


def eye_mask(n):
    return lax.broadcasted_iota(jnp.int32, (n, n), 0) == lax.broadcasted_iota(jnp.int32, (n, n), 1)


def above_mask(n):
    return lax.broadcasted_iota(jnp.int32, (n, n), 0) < lax.broadcasted_iota(jnp.int32, (n, n), 1)


class Plan:
    def __init__(self, nrow, ncol, width):
        self.ncol = ncol
        self.n = nrow * ncol
        self.parts = self.n // 4
        bits = [1 << b for b in range(1, self.n.bit_length() - 1)]
        y = [b for b in bits if b < ncol]
        x = [b for b in bits if ncol <= b < self.parts]
        self.z = [b for b in bits if b >= self.parts]
        self.stages = list(zip(x, y))
        tiles = width // TILE
        self.pairs = [(i, j) for i in range(tiles) for j in range(i + 1, tiles)]
        self.folds = [(i, i + 1) for i in range(0, tiles, 2)]
        self.diagonals = (len(self.pairs) + len(self.folds)) * TILE
        self.chunk = 8 * pl.cdiv(self.diagonals + 8, 8 * self.parts)
        self.half = self.chunk * self.parts // 2

    def me(self):
        return lax.axis_index("crow") * self.ncol + lax.axis_index("ccol")

    def rows(self, part, me):
        order = 0
        for mask in sum(self.stages, ()):
            here = jnp.bitwise_and(jnp.bitwise_xor(part, me), mask) // mask
            order = 2 * order + here
        return pl.ds(pl.multiple_of(order * self.chunk, 8), self.chunk)

    def halves(self, me, copy):
        for core in range(2):

            @pl.when(jnp.bitwise_and(me, 1) == core)
            def _():
                for part in range(self.parts):
                    copy(part, part & 1 == core)

    def swap(self, x, mask):
        return lax.ppermute(x, AXES, [(i, i ^ mask) for i in range(self.n)])


def gram_kernel(
    plan, sketch_ref, keep_ref, send_ref,
    rows_ref, flat, turned, whole, packed, load_sem,
):
    blocks = load_sem.shape[0]
    size = rows_ref.shape[0] // blocks
    width = rows_ref.shape[1]
    half = width // 2
    first, second = slice(0, half), slice(half, width)

    def load(i):
        at = pl.ds(i * size, size)
        return pltpu.make_async_copy(sketch_ref.at[at], rows_ref.at[at], load_sem.at[i])

    def prepare(i):
        if i != 1 and i & (i - 1) == 0:
            for j in range(i, min(max(2 * i, 2), blocks)):
                load(j).wait()
        h, l = split(rows_ref[i * size : (i + 1) * size, :])
        flat[2 * (i % 2)] = h
        flat[2 * (i % 2) + 1] = l
        turned[2 * (i % 2)] = h.T
        turned[2 * (i % 2) + 1] = l.T

    def push(slot, staged):
        pltpu.matmul_push_rhs(flat[slot, :, first], staged, 0)
        pltpu.matmul_push_rhs(flat[slot, :, second], staged, 1)

    for i in range(blocks):
        load(i).start()
    prepare(0)

    def sums(s00, z10, c00, z01, s11, c11):
        push(0, 0)
        for i in range(blocks):
            h, l = 2 * (i % 2), 2 * (i % 2) + 1
            push(l, 1)
            multiply(s00, turned[h, first, :], 0)
            multiply(s11, turned[h, second, :], 0)
            multiply(z10, turned[h, second, :])
            if i + 1 < blocks:
                prepare(i + 1)
                push(2 * ((i + 1) % 2), 0)
            multiply(s00, turned[l, first, :], 1)
            multiply(z01, turned[l, first, :], 1)
            multiply(c00, turned[h, first, :])
            multiply(z01, turned[h, first, :])
            multiply(z10, turned[h, second, :])
            multiply(s11, turned[l, second, :])
            multiply(c11, turned[h, second, :])

        cross = pltpu.matmul_pop(c00)
        whole[first, first] = pltpu.matmul_pop(s00) + cross + cross.T
        whole[first, second] = pltpu.matmul_pop(z01) + pltpu.matmul_pop(z10).T
        cross = pltpu.matmul_pop(c11)
        whole[second, second] = pltpu.matmul_pop(s11) + cross + cross.T

    square = (half, half)
    units = (0, 0, 0, 1, 1, 1)
    pl.run_scoped(sums, *[pltpu.ACC(unit)(square, F32) for unit in units])
    tile = lambda i, j: whole[i * TILE : (i + 1) * TILE, j * TILE : (j + 1) * TILE]
    packed[plan.diagonals :, :] = jnp.zeros_like(packed[plan.diagonals :, :])
    for t, (i, j) in enumerate(plan.pairs):
        packed[t * TILE : (t + 1) * TILE, :] = tile(i, j)
    for f, (i, j) in enumerate(plan.folds):
        t = len(plan.pairs) + f
        packed[t * TILE : (t + 1) * TILE, :] = jnp.where(above_mask(TILE), tile(i, i), tile(j, j))
        line = jnp.sum(jnp.where(eye_mask(TILE), tile(i, i), 0.0), axis=0, keepdims=True)
        packed[plan.diagonals + f : plan.diagonals + f + 1, :] = line
    me = plan.me()

    def copy(part, own):
        ref = keep_ref if own else send_ref
        ref[plan.rows(part, me), :] = packed[part * plan.chunk : (part + 1) * plan.chunk, :]

    plan.halves(me, copy)


def gram(plan, sketch):
    rows, width = sketch.shape
    half = width // 2
    return pl.pallas_call(
        functools.partial(gram_kernel, plan),
        in_specs=[pl.BlockSpec(memory_space=pl.ANY)],
        out_specs=[pl.BlockSpec(memory_space=pltpu.VMEM)] * 2,
        out_shape=[jax.ShapeDtypeStruct((plan.half, TILE), F32)] * 2,
        scratch_shapes=[
            pltpu.VMEM((rows, width), F32),
            pltpu.VMEM((4, half, width), BF16),
            pltpu.VMEM((4, width, half), BF16),
            pltpu.VMEM((width, width), F32),
            pltpu.VMEM((2 * plan.half, TILE), F32),
            pltpu.SemaphoreType.DMA((rows // half,)),
        ],
        compiler_params=pltpu.CompilerParams(vmem_limit_bytes=VMEM_LIMIT),
    )(sketch)


def share(plan, keep, send):
    own = keep + plan.swap(send, 1)
    for x, y in plan.stages:
        m = own.shape[0] // 4
        got = [plan.swap(own[d * m : (d + 1) * m], k) for d, k in ((1, y), (2, x), (3, x + y))]
        own = own[:m] + got[0] + got[1] + got[2]
    one, two = plan.z
    got = [plan.swap(own, z) for z in (one, two, one + two)]
    own = (own + got[0]) + (got[1] + got[2])
    pieces = [own]
    for x, y in reversed(plan.stages):
        got = [plan.swap(piece, mask) for mask in (y, x, x + y) for piece in pieces]
        pieces = pieces + got
    far = [plan.swap(piece, 1) for piece in pieces]
    return jnp.concatenate(pieces, axis=0), jnp.concatenate(far, axis=0)


def fold(x):
    n = x.shape[0]
    return jnp.sum(x.reshape(n // 8, 8, x.shape[1]), axis=0)


def near_inverse(accs, a, o_ref, y_ref, r1_ref, r2_ref, acc_ref):
    n = a.shape[0]
    eye = eye_mask(n)
    diagonal = jnp.where(eye, a, 0.0)
    s_row = lax.rsqrt(jnp.sum(diagonal, axis=0, keepdims=True))
    s_col = lax.rsqrt(jnp.sum(diagonal, axis=1, keepdims=True))
    c = a * s_col * s_row
    norm = jnp.max(jnp.sum(jnp.abs(c), axis=0, keepdims=True), axis=1, keepdims=True)
    inv_norm = 1.0 / norm
    rho0 = 1.0 - inv_norm
    start = jnp.where(eye, 1.0 - rho0, 0.0) - c * inv_norm
    o_ref[...] = start
    for ref in (y_ref, r1_ref, r2_ref):
        ref[...] = jnp.zeros((n, n), F32)
    acc_ref[...] = fold(jnp.where(eye, LOG1P[1] * (start + rho0), 0.0))
    square0, square1, factor0, factor1 = accs

    def more(carry):
        return jnp.logical_and(carry[0] < MAX_SQUARINGS, carry[1] >= 1e-3)

    def body(carry):
        k, _, rho, xi = carry
        o = o_ref[...]
        y = y_ref[...]
        oh, ol = split(o)
        yh, yl = split(y)
        sums_of(
            [(oh, [(square0, oh), (square0, ol), (factor0, yh)])],
            [(ol, [(square1, oh), (factor1, yh)]), (oh, [(factor1, yl)])],
        )
        r1 = r1_ref[...]
        r = o + jnp.where(eye, rho, 0.0)
        w0 = LOG1P[1] + LOG1P[2] + jnp.where(k >= 1, LOG1P[4], 0.0) + jnp.where(k >= 2, LOG1P[8], 0.0)
        w1 = jnp.where(k >= 1, LOG1P[3], 0.0) + jnp.where(k >= 2, LOG1P[6], 0.0)
        acc_ref[...] += fold(r * (w0 * r + w1 * r1 + LOG1P[5] * r2_ref[...]))
        size = jnp.sum(fold(r * r))
        r2_ref[...] = r1
        r1_ref[...] = r
        o_ref[...] = (2.0 * rho) * o + pop_both(square0, square1)
        y_ref[...] = (1.0 + rho) * y + xi * o + pop_both(factor0, factor1)
        return k + 1, size, rho * rho, xi * (1.0 + rho)

    begin = (jnp.int32(0), jnp.float32(1e30), jnp.max(rho0), jnp.max(inv_norm))
    _, size, _, xi = lax.while_loop(more, body, begin)
    x = y_ref[...] + jnp.where(eye, xi, 0.0)
    rest = jnp.where(eye, 1.0, 0.0) - dot6(accs, c, x)
    sums_of([(rest.astype(BF16), [(square0, x.astype(BF16))])])
    x = x + pltpu.matmul_pop(square0)
    log_det = n * jnp.log(norm) - jnp.sum(acc_ref[...], keepdims=True) - 2.0 * jnp.sum(
        jnp.log(s_row), axis=1, keepdims=True
    )
    return x * s_col * s_row, log_det, size


def sweep(a_ref, c_ref, log_ref):
    n = a_ref.shape[0]
    eye = eye_mask(n)
    diagonal = jnp.where(eye, a_ref[...], 0.0)
    s_row = lax.rsqrt(jnp.sum(diagonal, axis=0, keepdims=True))
    s_col = lax.rsqrt(jnp.sum(diagonal, axis=1, keepdims=True))
    c_ref[...] = a_ref[...] * s_col * s_row
    log_ref[...] = -2.0 * jnp.sum(jnp.log(s_row), axis=1, keepdims=True)
    lane = lax.broadcasted_iota(jnp.int32, (1, n), 1)

    @pl.loop(0, n)
    def _(k):
        row = c_ref[pl.ds(k, 1), :]
        here = lane == k
        pivot = jnp.sum(jnp.where(here, row, 0.0), axis=1, keepdims=True)
        log_ref[...] += jnp.log(pivot)
        u = jnp.where(here, pivot - 1.0, row)
        column = jnp.broadcast_to(u, (8, n)).T[:, :1]
        outer = column * (u / pivot)
        c_ref[...] = c_ref[...] - outer
        c_ref[pl.ds(k, 1), :] = c_ref[pl.ds(k, 1), :] - jnp.where(here, 2.0, 0.0)

    c_ref[...] = -(c_ref[...] * s_col * s_row)


def solve_kernel(
    plan, rows_all, near_ref, far_ref, sketch_ref, out_ref, log_ref,
    packed, a_ref, x_ref, o_ref, y_ref, r1_ref, r2_ref, acc_ref,
    rows_ref, result, mats, parts, load_sem, store_sem,
):
    blocks = load_sem.shape[0]
    size = rows_ref.shape[0] // blocks

    def load(i):
        at = pl.ds(i * size, size)
        return pltpu.make_async_copy(sketch_ref.at[at], rows_ref.at[at], load_sem.at[i])

    def store(i):
        at = pl.ds(i * size, size)
        return pltpu.make_async_copy(result.at[at], out_ref.at[at], store_sem.at[i])

    for i in range(blocks):
        load(i).start()

    n = a_ref.shape[0]
    m = n // 2
    me = plan.me()

    def copy(part, own):
        ref = near_ref if own else far_ref
        packed[part * plan.chunk : (part + 1) * plan.chunk, :] = ref[plan.rows(part, me), :]

    plan.halves(me, copy)

    scale = jnp.float32(1.0 / rows_all)
    unit = jnp.where(eye_mask(TILE), 1.0, 0.0)
    rows = lambda i: slice(i * TILE, (i + 1) * TILE)
    for t, (i, j) in enumerate(plan.pairs):
        tile = packed[rows(t), :] * scale
        a_ref[rows(i), rows(j)] = tile
        a_ref[rows(j), rows(i)] = tile.T
    above = above_mask(TILE)
    for f, (i, j) in enumerate(plan.folds):
        tile = packed[rows(len(plan.pairs) + f), :] * scale
        line = packed[plan.diagonals + f : plan.diagonals + f + 1, :] * scale
        mixed = jnp.where(eye_mask(TILE), line, jnp.where(above, tile, tile.T))
        a_ref[rows(i), rows(i)] = mixed + unit
        a_ref[rows(j), rows(j)] = jnp.where(above, tile.T, tile) + unit

    bufs = (o_ref, y_ref, r1_ref, r2_ref, acc_ref)

    def invert(*accs):
        x11, log1, size1 = near_inverse(accs, a_ref[:m, :m], *bufs)
        t12 = dot6(accs, x11, a_ref[:m, m:])
        schur = a_ref[m:, m:] - dot6(accs, a_ref[m:, :m], t12)
        x_ref[:m, :m] = x11
        x_ref[:m, m:] = t12
        x22, log2, size2 = near_inverse(accs, schur, *bufs)
        t12 = x_ref[:m, m:]
        x12 = -dot6(accs, t12, x22)
        x_ref[:m, :m] = x_ref[:m, :m] - dot6(accs, x12, t12.T)
        x_ref[:m, m:] = x12
        x_ref[m:, :m] = x12.T
        x_ref[m:, m:] = x22
        log_ref[...] = log1 + log2
        lost = jnp.max(jnp.sum(jnp.where(eye_mask(m), a_ref[m:, m:] - 32.0 * schur, 0.0), axis=0))
        good = jnp.logical_and(jnp.logical_and(size1 < 1e-3, size2 < 1e-3), lost <= 0.0)

        @pl.when(jnp.logical_not(good))
        def _():
            sweep(a_ref, x_ref, log_ref)

    pl.run_scoped(invert, *[pltpu.ACC(unit)((m, m), F32) for unit in (0, 1, 0, 1)])
    log_ref[...] = log_ref[...] / n
    eye = eye_mask(n)
    diagonal = jnp.sum(jnp.where(eye, x_ref[...], 0.0), axis=0, keepdims=True)
    high, low = split(jnp.where(eye, 0.0, x_ref[...]))
    mats[0] = high
    mats[1] = low
    for i in range(blocks):
        load(i).wait()

    def prepare(i):
        h, l = split(rows_ref[i * size : (i + 1) * size, :])
        parts[2 * (i % 2)] = h
        parts[2 * (i % 2) + 1] = l

    steps = [(i, k, which) for i in range(blocks) for k in range(2) for which in range(2)]

    def push(step):
        _, k, which = steps[step]
        for unit in range(2):
            tile = mats[which, k * m : (k + 1) * m, unit * m : (unit + 1) * m]
            pltpu.matmul_push_rhs(tile, which, unit)

    def products(*accs):
        def finish(i):
            at = slice(i * size, (i + 1) * size)
            for unit, acc in enumerate(accs[2 * (i % 2) : 2 * (i % 2) + 2]):
                cols = slice(unit * m, (unit + 1) * m)
                result[at, cols] = rows_ref[at, cols] * diagonal[:, cols] + pltpu.matmul_pop(acc)
            store(i).start()

        push(0)
        push(1)
        prepare(0)
        for step, (i, k, which) in enumerate(steps):
            h, l = 2 * (i % 2), 2 * (i % 2) + 1
            mine = accs[h : h + 2]
            cols = slice(k * m, (k + 1) * m)
            for acc in mine:
                multiply(acc, parts[h, :, cols], which)
            if which == 0:
                for acc in mine:
                    multiply(acc, parts[l, :, cols])
            if step + 2 < len(steps):
                push(step + 2)
            if k == 0 and which == 0 and i > 0:
                finish(i - 1)
            if k == 0 and which == 1 and i + 1 < blocks:
                prepare(i + 1)
        finish(blocks - 1)

    pl.run_scoped(products, *[pltpu.ACC(unit)((size, m), F32) for unit in (0, 1, 0, 1)])
    for i in range(blocks):
        store(i).wait()


def solve(plan, sketch, near, far):
    rows, width = sketch.shape
    m = width // 2
    block = min(512, rows)
    vmem = pl.BlockSpec(memory_space=pltpu.VMEM)
    hbm = pl.BlockSpec(memory_space=pl.ANY)
    return pl.pallas_call(
        functools.partial(solve_kernel, plan, rows * plan.n),
        in_specs=[vmem, vmem, hbm],
        out_specs=[hbm, vmem],
        out_shape=[
            jax.ShapeDtypeStruct((rows, width), F32),
            jax.ShapeDtypeStruct((1, 1), F32),
        ],
        scratch_shapes=[
            pltpu.VMEM((2 * plan.half, TILE), F32),
            pltpu.VMEM((width, width), F32),
            pltpu.VMEM((width, width), F32),
            pltpu.VMEM((m, m), F32),
            pltpu.VMEM((m, m), F32),
            pltpu.VMEM((m, m), F32),
            pltpu.VMEM((m, m), F32),
            pltpu.VMEM((8, m), F32),
            pltpu.VMEM((rows, width), F32),
            pltpu.VMEM((rows, width), F32),
            pltpu.VMEM((2, width, width), BF16),
            pltpu.VMEM((4, block, width), BF16),
            pltpu.SemaphoreType.DMA((rows // block,)),
            pltpu.SemaphoreType.DMA((rows // block,)),
        ],
        compiler_params=pltpu.CompilerParams(vmem_limit_bytes=VMEM_LIMIT),
    )(near, far, sketch)


def solution(mesh):
    nrow, ncol = mesh.shape["crow"], mesh.shape["ccol"]

    def on_device(sketch):
        plan = Plan(nrow, ncol, sketch.shape[1])
        keep, send = gram(plan, sketch)
        near, far = share(plan, keep, send)
        basis, log_mean = solve(plan, sketch, near, far)
        return basis, log_mean[0, 0]

    return jax.shard_map(
        on_device,
        mesh=mesh,
        in_specs=(P(AXES, None),),
        out_specs=(P(AXES, None), P()),
        check_vma=False,
    )
```
